128 devices in a mesh: leaf: 32 (over z, x, core), grp: 4 (over y).
Axes of the slice: x: 4, y: 4, z: 4, core: 2. Of those that a mesh axis runs over, the one named last changes fastest.
Arguments:
- signal: float32 [32, 262144], P(None, ('leaf', 'grp')), may hold values from -6 to 6
- near_index: int32 [1024, 4], P(('leaf', 'grp')), may hold values from 0 to 1023, as said below
- near_block: float32 [1024, 4, 256, 256], P(('leaf', 'grp')), may hold values from -0.1875 to 0.1875
- basis: float32 [1024, 256, 64], P(('leaf', 'grp')), may hold values from -0.375 to 0.375
- far0_index: int32 [1024, 8], P(('leaf', 'grp')), may hold values from 0 to 1023, as said below
- coupling0: float32 [1024, 8, 64, 64], P(('leaf', 'grp')), may hold values from -0.25 to 0.25
- transfer1: float32 [1024, 64, 64], P(('leaf', 'grp')), may hold values from -0.25 to 0.25
- transfer2: float32 [128, 64, 64], P(('leaf', 'grp')), may hold values from -0.375 to 0.375
- far1_index: int32 [128, 8], P(('leaf', 'grp')), may hold values from 0 to 127, as said below
- coupling1: float32 [128, 8, 64, 64], P(('leaf', 'grp')), may hold values from -0.25 to 0.25
- far2_index: int32 [32, 8], P('leaf'), may hold values from 0 to 31, as said below
- coupling2: float32 [32, 8, 64, 64], P('leaf'), may hold values from -0.25 to 0.25
Outputs:
- first_image: float32 [32, 262144], P(None, ('leaf', 'grp'))
- second_image: float32 [32, 262144], P(None, ('leaf', 'grp'))
The draws below stay inside these ranges and needn't reach their ends.
Inputs may be any that keep to these rules, and one draw needn't show every extreme that they name: `near_index`: row l lists leaves within 8 of l; its first entry is l itself and its second lies at distance exactly 8. `far0_index`: row l lists leaves within 8 of l; its first entry lies at distance exactly 8. `far1_index`: any device clusters; the first column names each device cluster once. `far2_index`: any group clusters; the first column names each group cluster once.
All inputs are finite; a program needn't handle non-finite values.
Results may differ from the reference program's by a relative error of at most 0.000096.
Values sent between devices are 32-bit elements; how exact they have to be, the bound alone decides.
A program may use at most 64 MiB of HBM per device.

```python
import jax
import jax.numpy as jnp
from jax import lax

NODE = 256
RANK = 64
RHS = 32
LEAF_DEV = 8
NEAR = 4
FAR0 = 8
FAR1 = 8
FAR2 = 8
LEAVES = 1024
POINTS = 262144
GROUPS = 32
N_GRP = 4
DEVICES = 128


def nearby_leaves(key, count, reach, total, self_first):
    rows = jnp.arange(total, dtype=jnp.int32)[:, None]
    offsets = jax.random.randint(key, (total, count), -reach, reach + 1).astype(jnp.int32)
    signs = jax.random.randint(jax.random.fold_in(key, 1), (total, 1), 0, 2).astype(jnp.int32) * 2 - 1
    column = jnp.arange(count, dtype=jnp.int32)[None, :]
    if self_first:
        offsets = jnp.where(column == 0, 0, offsets)
        offsets = jnp.where(column == 1, signs * reach, offsets)
    else:
        offsets = jnp.where(column == 0, signs * reach, offsets)
    target = rows + offsets
    target = jnp.where((target < 0) | (target >= total), rows - offsets, target)
    return target.astype(jnp.int32)


def cluster_lists(key, total, count):
    first = jax.random.permutation(key, total).astype(jnp.int32)[:, None]
    others = jax.random.randint(jax.random.fold_in(key, 1), (total, count - 1), 0, total).astype(jnp.int32)
    return jnp.concatenate([first, others], axis=1)


def draw_near_index(key, part):
    key = jax.random.fold_in(key, 11)
    return nearby_leaves(key, NEAR, LEAF_DEV, LEAVES, True)


def draw_far0_index(key, part):
    key = jax.random.fold_in(key, 12)
    return nearby_leaves(key, FAR0, LEAF_DEV, LEAVES, False)


def draw_far1_index(key, part):
    key = jax.random.fold_in(key, 13)
    return cluster_lists(key, DEVICES, FAR1)


def draw_far2_index(key, part):
    key = jax.random.fold_in(key, 14)
    return cluster_lists(key, GROUPS, FAR2)


def block_scale(rng, shape, shards, low, top_value):
    level, own = 1.0, jax.random.fold_in(rng, 6)
    for position, shards_of in shards:
        steps = jnp.exp(jax.random.uniform(jax.random.fold_in(own, position), (shards_of,), jnp.float32, low / len(shards), top_value / len(shards)))
        level = level * jnp.repeat(steps, shape[position] // shards_of).reshape([-1 if axis == position else 1 for axis in range(len(shape))])
    return level


def scatter_about(own_key, dims, spread, most, split=(), held_as=jnp.bfloat16):
    values = spread * jax.random.normal(own_key, dims, jnp.float32)
    if split:
        values = values * block_scale(own_key, dims, split, -0.22, 0.18)
    return jnp.clip(values, -most, most).astype(held_as)


def setup_inputs(seed: int = 0) -> dict:
    splits = jax.random.split(jax.random.key(seed), 13)
    signal = scatter_about(splits[0], (RHS, POINTS), 1.0, 6.0, ((1, 128),), jnp.float32)
    near_index = draw_near_index(jax.random.fold_in(splits[12], 71), 0)
    near_block = scatter_about(splits[2], (LEAVES, NEAR, NODE, NODE), (NODE * NEAR) ** -0.5, 0.1875, ((0, 128),), jnp.float32)
    basis = scatter_about(splits[3], (LEAVES, NODE, RANK), NODE ** -0.5, 0.375, ((0, 128),), jnp.float32)
    far0_index = draw_far0_index(jax.random.fold_in(splits[12], 71), 0)
    coupling0 = scatter_about(splits[5], (LEAVES, FAR0, RANK, RANK), (RANK * FAR0) ** -0.5, 0.25, ((0, 128),), jnp.float32)
    transfer1 = scatter_about(splits[6], (LEAVES, RANK, RANK), (RANK * LEAF_DEV) ** -0.5, 0.25, ((0, 128),), jnp.float32)
    transfer2 = scatter_about(splits[7], (DEVICES, RANK, RANK), (RANK * N_GRP) ** -0.5, 0.375, ((0, 128),), jnp.float32)
    far1_index = draw_far1_index(jax.random.fold_in(splits[12], 71), 0)
    coupling1 = scatter_about(splits[9], (DEVICES, FAR1, RANK, RANK), (RANK * FAR1) ** -0.5, 0.25, ((0, 128),), jnp.float32)
    far2_index = draw_far2_index(jax.random.fold_in(splits[12], 71), 0)
    coupling2 = scatter_about(splits[11], (GROUPS, FAR2, RANK, RANK), (RANK * FAR2) ** -0.5, 0.25, ((0, 32),), jnp.float32)
    return {"signal": signal, "near_index": near_index, "near_block": near_block, "basis": basis, "far0_index": far0_index, "coupling0": coupling0, "transfer1": transfer1, "transfer2": transfer2, "far1_index": far1_index, "coupling1": coupling1, "far2_index": far2_index, "coupling2": coupling2}


HIGHEST_MODE = lax.Precision.HIGHEST


def apply_kernel(signal, near_index, near_block, basis, far0_index, coupling0, transfer1, transfer2, far1_index, coupling1, far2_index, coupling2):
    leaf_total = basis.shape[0]
    device_total = transfer2.shape[0]
    fields = signal.reshape(RHS, leaf_total, NODE)
    leaf_coefs = jnp.einsum('lnq,sln->slq', basis, fields, precision=HIGHEST_MODE)
    cluster = jnp.einsum('dmrq,sdmr->dqs', transfer1.reshape(device_total, LEAF_DEV, RANK, RANK), leaf_coefs.reshape(RHS, device_total, LEAF_DEV, RANK), precision=HIGHEST_MODE)
    lifted = jnp.einsum('drq,drs->dqs', transfer2, cluster, precision=HIGHEST_MODE)
    coarse = lifted.reshape(GROUPS, N_GRP, RANK, RHS).sum(axis=1)
    far_top = jnp.einsum('gkqr,gkrs->gqs', coupling2, coarse[far2_index], precision=HIGHEST_MODE)
    far_mid = jnp.einsum('dkqr,dkrs->dqs', coupling1, cluster[far1_index], precision=HIGHEST_MODE)
    owner_group = (jnp.arange(device_total) // N_GRP).astype(jnp.int32)
    down_mid = jnp.einsum('dqr,drs->dqs', transfer2, far_top[owner_group], precision=HIGHEST_MODE) + far_mid
    far_leaf = jnp.einsum('lkqr,slkr->slq', coupling0, leaf_coefs[:, far0_index], precision=HIGHEST_MODE)
    owner_device = (jnp.arange(leaf_total) // LEAF_DEV).astype(jnp.int32)
    down_leaf = jnp.einsum('lqr,lrs->slq', transfer1, down_mid[owner_device], precision=HIGHEST_MODE) + far_leaf
    result = jnp.einsum('lnq,slq->sln', basis, down_leaf, precision=HIGHEST_MODE)
    result = result + jnp.einsum('lkmn,slkn->slm', near_block, fields[:, near_index], precision=HIGHEST_MODE)
    return result.reshape(RHS, leaf_total * NODE)


def reference(signal, near_index, near_block, basis, far0_index, coupling0, transfer1, transfer2, far1_index, coupling1, far2_index, coupling2):
    first_image = apply_kernel(signal, near_index, near_block, basis, far0_index, coupling0, transfer1, transfer2, far1_index, coupling1, far2_index, coupling2)
    second_image = apply_kernel(first_image, near_index, near_block, basis, far0_index, coupling0, transfer1, transfer2, far1_index, coupling1, far2_index, coupling2)
    return first_image, second_image
```

```python
import math

import jax
import jax.numpy as jnp
from jax import lax
from jax.experimental import pallas as pl
from jax.experimental.pallas import tpu as pltpu
from jax.sharding import PartitionSpec as P

F32 = jnp.float32
BF16 = jnp.bfloat16
MESH = pl.DeviceIdType.MESH
LEAF = 8
NODE = 256
RANK = 64
RHS = 32
NEAR = 4
FAR = 8
WIDE = RANK * FAR


def dot_nt(a, b):
    return lax.dot_general(a, b, (((1,), (1,)), ((), ())), preferred_element_type=F32)


def dot_nn(a, b):
    return lax.dot_general(a, b, (((1,), (0,)), ((), ())), preferred_element_type=F32)


def dot_full(a, b, dim=1):
    return lax.dot_general(
        a, b, (((dim,), (0,)), ((), ())), precision=lax.Precision.HIGHEST, preferred_element_type=F32
    )


def split(t):
    hi = t.astype(BF16)
    return hi, (t - hi.astype(F32)).astype(BF16)


def stacked(t):
    return jnp.concatenate(split(t), axis=0)


def product(dot, x, wh, wl):
    r = dot(x, wh)
    return r[:RHS] + r[RHS:] + dot(x[:RHS], wl)


def swap(t):
    return pltpu.roll(t, RANK, 1)


def kernel(
    ZN, XN, YN,
    signal, near_index, near_block, basis, far0_index, coupling0, transfer1, transfer2,
    far1_index, coupling1, far2_index, coupling2,
    first, second,
    fld, xs, hf, na, ah, al, bs, t1, t2, c0, c0h, c0l, c1s, c2s, c1f, c1h, c1l, c2f, c2h, c2l,
    yb, cba, cbb, gba, gbb, psx, pbx, psz, pbz, lcs, lch, lcd, acc, ft, si1, si2,
    in_sem, sig_sem, near_sem, out_sem, hs, hr, es, er, ys, yr, zs, zr, gs, gr, fs, fr,
    pxs, pxr, pzs, pzr, k1s, k1r, k2s, k2r, i1s, i1r, i2s, i2r,
):
    leaf = lax.axis_index("leaf")
    y = lax.axis_index("grp")
    c = lax.rem(leaf, 2)
    x = lax.rem(leaf // 2, XN)
    z = leaf // (2 * XN)
    leaves = 2 * XN * ZN
    cb, gb = (cba, cbb), (gba, gbb)
    lane = lax.broadcasted_iota(jnp.int32, (RHS, 2 * RANK), 1)
    low = lane < RANK

    def at(zz, xx, cc, yy):
        return ((zz * XN + xx) * 2 + cc, yy)

    y_peers = [lax.rem(y + o, YN) for o in range(1, YN)]
    x_peers = [lax.rem(x + o, XN) for o in range(1, XN)]
    z_peers = [lax.rem(z + o, ZN) for o in range(1, ZN)]
    sibling = at(z, x, 1 - c, y)
    after = (lax.rem(leaf + (y + 1) // YN, leaves), lax.rem(y + 1, YN))
    before = (lax.rem(leaf + leaves - 1 + (y + YN - 1) // YN, leaves), lax.rem(y + YN - 1, YN))

    def remote(src, dst, ssem, rsem, dev):
        return pltpu.make_async_remote_copy(
            src_ref=src, dst_ref=dst, send_sem=ssem, recv_sem=rsem, device_id=dev, device_id_type=MESH
        )

    loads = []
    for n, (src, dst) in enumerate((
        (coupling1.at[0], c1s), (coupling2.at[0], c2s), (basis, bs), (transfer1, t1), (transfer2.at[0], t2),
        (coupling0, c0), (far1_index, si1.at[x]), (far2_index, si2.at[z]),
    )):
        loads.append(pltpu.make_async_copy(src, dst, in_sem.at[n]))
    for i in range(LEAF):
        pltpu.make_async_copy(signal.at[:, pl.ds(i * NODE, NODE)], fld.at[0, i], sig_sem.at[i]).start()
    for cp in loads:
        cp.start()

    def near_load(l):
        return pltpu.make_async_copy(near_block.at[l], na.at[l], near_sem.at[l])

    for l in range(LEAF):
        near_load(l).start()

    greet = [at(z, x, c, yy) for yy in y_peers] + [at(z, xx, c, y) for xx in x_peers]
    greet += [at(zz, x, c, y) for zz in z_peers] + [sibling, after, before]
    barrier = pltpu.get_barrier_semaphore()
    for dev in greet:
        pl.semaphore_signal(barrier, inc=1, device_id=dev, device_id_type=MESH)
    pl.semaphore_wait(barrier, len(greet))

    def halo(p, side, i):
        return remote(
            fld.at[p, i], hf.at[p, side, i], hs.at[p, side, i], hr.at[p, side, i], after if side == 0 else before
        )

    def send_halo(p):
        for i in range(LEAF):
            halo(p, 0, LEAF - 1 - i).start()
            halo(p, 1, i).start()

    for i in range(LEAF):
        pltpu.make_async_copy(signal.at[:, pl.ds(i * NODE, NODE)], fld.at[0, i], sig_sem.at[i]).wait()
    send_halo(0)

    def coupling_copies():
        out = [
            (remote(c1f.at[x], c1f.at[x], k1s.at[xx], k1r.at[x], at(z, xx, c, y)),
             remote(si1.at[x], si1.at[x], i1s.at[xx], i1r.at[x], at(z, xx, c, y)))
            for xx in x_peers
        ]
        out += [
            (remote(c2f.at[z], c2f.at[z], k2s.at[zz], k2r.at[z], at(zz, x, c, y)),
             remote(si2.at[z], si2.at[z], i2s.at[zz], i2r.at[z], at(zz, x, c, y)))
            for zz in z_peers
        ]
        return out

    for cp in loads:
        cp.wait()
    for j in range(FAR // 2):
        c1f[x, :, pl.ds(2 * j * RANK, 2 * RANK)] = jnp.concatenate([c1s[2 * j], c1s[2 * j + 1]], axis=1)
        c2f[z, :, pl.ds(2 * j * RANK, 2 * RANK)] = jnp.concatenate([c2s[2 * j], c2s[2 * j + 1]], axis=1)
    for pair in coupling_copies():
        for cp in pair:
            cp.start()

    row = lax.broadcasted_iota(jnp.int32, (RANK, 2 * RANK), 0)
    col = lax.broadcasted_iota(jnp.int32, (RANK, 2 * RANK), 1)
    eye = (row == col).astype(F32)

    def fold(l, carry):
        tl = t1[l]
        e = jnp.concatenate([jnp.concatenate([tl, dot_full(tl, t2[...])], axis=1), eye], axis=1)
        hi, lo = split(dot_full(e, bs[l], 0))
        ah[l, NEAR] = hi
        al[l, NEAR] = lo
        xs[LEAF + l] = stacked(fld[0, l])
        ft[l] = jnp.zeros((RHS, NODE), F32)
        xs[l] = jnp.zeros((2 * RHS, NODE), BF16)
        xs[2 * LEAF + l] = jnp.zeros((2 * RHS, NODE), BF16)
        return carry

    lax.fori_loop(0, LEAF, fold, 0)

    base = (leaf * YN + y) * LEAF - LEAF

    def near_split(l, carry):
        near_load(l).wait()
        for k in range(NEAR):
            hi, lo = split(na[l, k])
            ah[l, k] = hi
            al[l, k] = lo
        return carry

    def near_own(l, carry):
        acc[l] = product(dot_nt, xs[LEAF + l], ah[l, 0], al[l, 0])
        return carry

    def coupling_split(l, carry):
        for j in range(FAR // 2):
            hi, lo = split(jnp.concatenate([c0[l, 2 * j], c0[l, 2 * j + 1]], axis=1))
            c0h[l, :, pl.ds(2 * j * RANK, 2 * RANK)] = hi
            c0l[l, :, pl.ds(2 * j * RANK, 2 * RANK)] = lo
        return carry

    def coef_copy(p, side):
        return remote(lcs.at[p], lch.at[p, side], es.at[p, side], er.at[p, side], after if side == 0 else before)

    def y_copy(p, yy):
        return remote(yb.at[p, y], yb.at[p, y], ys.at[p, yy], yr.at[p, y], at(z, x, c, yy))

    def y_wait(p, yy):
        remote(yb.at[p, yy], yb.at[p, yy], ys.at[p, yy], yr.at[p, yy], at(z, x, c, yy)).wait_recv()

    def z_copy(p, zz, slot):
        return remote(cb[p].at[0, slot], cb[p].at[0, slot], zs.at[p, zz], zr.at[p, slot], at(zz, x, c, y))

    def g_copy(p, xx, slot):
        return remote(gb[p].at[0, slot], gb[p].at[0, slot], gs.at[p, xx], gr.at[p, slot], at(z, xx, c, y))

    def forward(p):
        return (
            remote(cb[p].at[0], cb[p].at[1], fs.at[p, 0], fr.at[p, 0], sibling),
            remote(gb[p].at[0], gb[p].at[1], fs.at[p, 1], fr.at[p, 1], sibling),
        )

    def px_copy(p, xx, slot):
        return remote(psx.at[p, xx], pbx.at[p, slot], pxs.at[p, xx], pxr.at[p, slot], at(z, xx, c, y))

    def pz_copy(p, zz, slot):
        return remote(psz.at[p, zz], pbz.at[p, slot], pzs.at[p, zz], pzr.at[p, slot], at(zz, x, c, y))

    def wide(i):
        return jnp.minimum(jnp.maximum(i - base, 0), 3 * LEAF - 1)

    def slot_of(cc):
        return jnp.where(cc == c, 0, 1)

    def mid_tile(p, m, k):
        i = si1[m, 0, k]
        yy = lax.rem(i, YN)
        g = lax.div(i, YN)
        cc = lax.rem(g, 2)
        xx = lax.rem(lax.div(g, 2), XN)
        zz = lax.div(g, 2 * XN)
        t = cb[p][slot_of(cc), zz, lax.div(yy, 2)]
        t = jnp.where(lax.rem(yy, 2) == k % 2, t, swap(t))
        return jnp.where(xx == x, t, 0.0)

    def top_tile(p, m, k):
        i = si2[m, 0, k]
        cc = lax.rem(i, 2)
        xx = lax.rem(lax.div(i, 2), XN)
        zz = lax.div(i, 2 * XN)
        return jnp.where(zz == z, gb[p][slot_of(cc), xx], 0.0)

    def leaf_tile(l, k):
        return lcd[wide(far0_index[l, k])]

    def picked(tile):
        return jnp.concatenate(
            [stacked(jnp.where(low, tile(2 * j), tile(2 * j + 1))) for j in range(FAR // 2)], axis=1
        )

    nothing = jnp.zeros((RHS, RANK), F32)

    def apply(p):
        def up(j, u):
            ra = product(dot_nt, xs[LEAF + 2 * j], ah[2 * j, NEAR], al[2 * j, NEAR])
            rb = product(dot_nt, xs[LEAF + 2 * j + 1], ah[2 * j + 1, NEAR], al[2 * j + 1, NEAR])
            la, lb = ra[:, 2 * RANK:], rb[:, 2 * RANK:]
            lcs[p, j] = la + swap(lb)
            lcd[LEAF + 2 * j] = la + swap(la)
            lcd[LEAF + 2 * j + 1] = lb + swap(lb)
            return u + ra[:, :2 * RANK] + rb[:, :2 * RANK]

        yb[p, y] = lax.fori_loop(0, LEAF // 2, up, jnp.zeros((RHS, 2 * RANK), F32))
        for yy in y_peers:
            y_copy(p, yy).start()
        for side in range(2):
            coef_copy(p, side).start()
        if p == 1:
            send_halo(1)
        else:
            lax.fori_loop(0, LEAF, near_split, 0)
        lax.fori_loop(0, LEAF, near_own, 0)

        for yy in y_peers:
            y_wait(p, yy)
        for j in range(YN // 2):
            cb[p][0, z, j] = jnp.where(low, yb[p, 2 * j], swap(yb[p, 2 * j + 1]))
        total = yb[p, 0]
        for i in range(1, YN):
            total = total + yb[p, i]
        gb[p][0, x] = jnp.where(low, swap(total), total)
        for zz in z_peers:
            z_copy(p, zz, z).start()
        for xx in x_peers:
            g_copy(p, xx, x).start()

        if p == 0:
            lax.fori_loop(0, LEAF, coupling_split, 0)
        for side in range(2):
            coef_copy(p, side).wait_recv()

        def unpack(j, carry):
            for side in range(2):
                t = lch[p, side, j]
                r = swap(t)
                lcd[side * 2 * LEAF + 2 * j] = jnp.where(low, t, r)
                lcd[side * 2 * LEAF + 2 * j + 1] = jnp.where(low, r, t)
            return carry

        lax.fori_loop(0, LEAF // 2, unpack, 0)

        def far_leaf(l, carry):
            v = product(dot_nt, picked(lambda k: leaf_tile(l, k)), c0h[l], c0l[l])
            ft[l, :, pl.ds(2 * RANK, RANK)] = v
            return carry

        lax.fori_loop(0, LEAF, far_leaf, 0)

        for zz in z_peers:
            z_copy(p, zz, zz).wait_recv()
        for xx in x_peers:
            g_copy(p, xx, xx).wait_recv()
        fw = forward(p)
        for cp in fw:
            cp.start()
        if p == 0:
            for xx in x_peers:
                remote(c1f.at[xx], c1f.at[xx], k1s.at[xx], k1r.at[xx], at(z, xx, c, y)).wait_recv()
                remote(si1.at[xx], si1.at[xx], i1s.at[xx], i1r.at[xx], at(z, xx, c, y)).wait_recv()
            for zz in z_peers:
                remote(c2f.at[zz], c2f.at[zz], k2s.at[zz], k2r.at[zz], at(zz, x, c, y)).wait_recv()
                remote(si2.at[zz], si2.at[zz], i2s.at[zz], i2r.at[zz], at(zz, x, c, y)).wait_recv()
            for m in range(XN):
                c1h[m], c1l[m] = split(c1f[m])
            for m in range(ZN):
                c2h[m], c2l[m] = split(c2f[m])
        for cp in fw:
            cp.wait_recv()

        def part_x(m, carry):
            v = product(dot_nt, picked(lambda k: mid_tile(p, m, k)), c1h[m], c1l[m])
            psx[p, m] = jnp.concatenate([v, nothing], axis=1)
            return carry

        def part_z(m, carry):
            v = product(dot_nt, picked(lambda k: top_tile(p, m, k)), c2h[m], c2l[m])
            psz[p, m] = jnp.concatenate([nothing, v], axis=1)
            return carry

        lax.fori_loop(0, XN, part_x, 0)
        for xx in x_peers:
            px_copy(p, xx, x).start()
        lax.fori_loop(0, ZN, part_z, 0)
        for zz in z_peers:
            pz_copy(p, zz, z).start()

        def take(side, i):
            halo(p, side, i).wait_recv()
            xs[side * 2 * LEAF + i] = stacked(hf[p, side, i])

        def near_leaf(l):
            total = acc[l]
            for k in range(1, NEAR):
                total = total + product(dot_nt, xs[wide(near_index[k, l])], ah[l, k], al[l, k])
            acc[l] = total

        half = LEAF // 2

        def take_first(i, carry):
            take(0, LEAF - 1 - i)
            take(1, i)
            return carry

        lax.fori_loop(0, half, take_first, 0)

        def near_pair(j, carry):
            take(0, half - 1 - j)
            take(1, half + j)
            near_leaf(half - 1 - j)
            near_leaf(half + j)
            return carry

        lax.fori_loop(0, half, near_pair, 0)

        for xx in x_peers:
            px_copy(p, xx, xx).wait_recv()
        for zz in z_peers:
            pz_copy(p, zz, zz).wait_recv()
        down = psx[p, x] + psz[p, z]
        for xx in x_peers:
            down = down + pbx[p, xx]
        for zz in z_peers:
            down = down + pbz[p, zz]

        def finish(l, carry):
            ft[l, :, pl.ds(0, 2 * RANK)] = down
            v = acc[l] + product(dot_nn, stacked(ft[l]), ah[l, NEAR], al[l, NEAR])
            fld[p + 1, l] = v
            if p == 0:
                xs[LEAF + l] = stacked(v)
            return carry

        lax.fori_loop(0, LEAF, finish, 0)
        out = first if p == 0 else second
        for l in range(LEAF):
            pltpu.make_async_copy(fld.at[p + 1, l], out.at[:, pl.ds(l * NODE, NODE)], out_sem.at[p, l]).start()

    apply(0)
    apply(1)

    for pair in coupling_copies():
        for cp in pair:
            cp.wait_send()
    for p in range(2):
        for side in range(2):
            for i in range(LEAF):
                halo(p, side, i).wait_send()
            coef_copy(p, side).wait_send()
        for yy in y_peers:
            y_copy(p, yy).wait_send()
        for zz in z_peers:
            z_copy(p, zz, z).wait_send()
            pz_copy(p, zz, z).wait_send()
        for xx in x_peers:
            g_copy(p, xx, x).wait_send()
            px_copy(p, xx, x).wait_send()
        for cp in forward(p):
            cp.wait_send()
        out = first if p == 0 else second
        for l in range(LEAF):
            pltpu.make_async_copy(fld.at[p + 1, l], out.at[:, pl.ds(l * NODE, NODE)], out_sem.at[p, l]).wait()


def solution(mesh):
    leaf, grp = ("leaf", "grp")
    YN = mesh.shape[grp]
    XN = ZN = math.isqrt(mesh.shape[leaf] // 2)
    both = (leaf, grp)
    placed = (
        P(None, both),
        P(both, None),
        P(both, None, None, None),
        P(both, None, None),
        P(both, None),
        P(both, None, None, None),
        P(both, None, None),
        P(both, None, None),
        P(both, None),
        P(both, None, None, None),
        P(leaf, None),
        P(leaf, None, None, None),
    )

    def body(*refs):
        return kernel(ZN, XN, YN, *refs)

    hbm = pl.BlockSpec(memory_space=pl.ANY)
    smem = pl.BlockSpec(memory_space=pltpu.SMEM)
    vmem = pltpu.VMEM
    dma = pltpu.SemaphoreType.DMA
    cols = LEAF * NODE
    scratch = [
        vmem((3, LEAF, RHS, NODE), F32),
        vmem((3 * LEAF, 2 * RHS, NODE), BF16),
        vmem((2, 2, LEAF, RHS, NODE), F32),
        vmem((LEAF, NEAR, NODE, NODE), F32),
        vmem((LEAF, NEAR + 1, NODE, NODE), BF16),
        vmem((LEAF, NEAR + 1, NODE, NODE), BF16),
        vmem((LEAF, RANK, NODE), F32),
        vmem((LEAF, RANK, RANK), F32),
        vmem((RANK, RANK), F32),
        vmem((LEAF, FAR, RANK, RANK), F32),
        vmem((LEAF, RANK, WIDE), BF16),
        vmem((LEAF, RANK, WIDE), BF16),
        vmem((FAR, RANK, RANK), F32),
        vmem((FAR, RANK, RANK), F32),
        vmem((XN, RANK, WIDE), F32),
        vmem((XN, RANK, WIDE), BF16),
        vmem((XN, RANK, WIDE), BF16),
        vmem((ZN, RANK, WIDE), F32),
        vmem((ZN, RANK, WIDE), BF16),
        vmem((ZN, RANK, WIDE), BF16),
        vmem((2, YN, RHS, 2 * RANK), F32),
        vmem((2, ZN, YN // 2, RHS, 2 * RANK), F32),
        vmem((2, ZN, YN // 2, RHS, 2 * RANK), F32),
        vmem((2, XN, RHS, 2 * RANK), F32),
        vmem((2, XN, RHS, 2 * RANK), F32),
        vmem((2, XN, RHS, 2 * RANK), F32),
        vmem((2, XN, RHS, 2 * RANK), F32),
        vmem((2, ZN, RHS, 2 * RANK), F32),
        vmem((2, ZN, RHS, 2 * RANK), F32),
        vmem((2, LEAF // 2, RHS, 2 * RANK), F32),
        vmem((2, 2, LEAF // 2, RHS, 2 * RANK), F32),
        vmem((3 * LEAF, RHS, 2 * RANK), F32),
        vmem((LEAF, RHS, NODE), F32),
        vmem((LEAF, RHS, NODE), F32),
        pltpu.SMEM((XN, 1, FAR), jnp.int32),
        pltpu.SMEM((ZN, 1, FAR), jnp.int32),
        dma((8,)), dma((LEAF,)), dma((LEAF,)), dma((2, LEAF)),
        dma((2, 2, LEAF)), dma((2, 2, LEAF)),
        dma((2, 2)), dma((2, 2)),
        dma((2, YN)), dma((2, YN)),
        dma((2, ZN)), dma((2, ZN)),
        dma((2, XN)), dma((2, XN)),
        dma((2, 2)), dma((2, 2)),
        dma((2, XN)), dma((2, XN)),
        dma((2, ZN)), dma((2, ZN)),
        dma((XN,)), dma((XN,)), dma((ZN,)), dma((ZN,)),
        dma((XN,)), dma((XN,)), dma((ZN,)), dma((ZN,)),
    ]

    def per_device(signal, near_index, near_block, basis, *rest):
        args = (signal, near_index.T, near_block, jnp.swapaxes(basis, 1, 2), *rest)
        call = pl.pallas_call(
            body,
            out_shape=[jax.ShapeDtypeStruct((RHS, cols), F32)] * 2,
            in_specs=[hbm, smem, hbm, hbm, smem] + [hbm] * 7,
            out_specs=[hbm, hbm],
            scratch_shapes=scratch,
            compiler_params=pltpu.CompilerParams(
                collective_id=0, has_side_effects=True, vmem_limit_bytes=56 * 1024 * 1024
            ),
        )
        return tuple(call(*args))

    return jax.shard_map(
        per_device,
        mesh=mesh,
        in_specs=placed,
        out_specs=(P(None, both), P(None, both)),
        check_vma=False,
    )
```

```python
import math

import jax
import jax.numpy as jnp
from jax import lax
from jax.experimental import pallas as pl
from jax.experimental.pallas import tpu as pltpu
from jax.sharding import PartitionSpec as P

F32 = jnp.float32
BF16 = jnp.bfloat16
MESH = pl.DeviceIdType.MESH
LEAF = 8
NODE = 256
RANK = 64
RHS = 32
NEAR = 4
FAR = 8
WIDE = RANK * FAR
PACK = RHS // 2
LANES = 2 * RANK


def dot(a, b, da, db):
    return lax.dot_general(a, b, (((da,), (db,)), ((), ())), preferred_element_type=F32)


def dot_nt(a, b):
    return dot(a, b, 1, 1)


def dot_nn(a, b):
    return dot(a, b, 1, 0)


def dot_tn(a, b):
    return dot(a, b, 0, 0)


def split(t):
    hi = t.astype(BF16)
    return hi, (t - hi.astype(F32)).astype(BF16)


def stacked(t):
    return jnp.concatenate(split(t), axis=0)


def product(f, x, wh, wl):
    r = f(x, wh)
    return r[:RHS] + r[RHS:] + f(x[:RHS], wl)


def three(f, a, b):
    return f(a[0], b[0]) + f(a[1], b[0]) + f(a[0], b[1])


def swap(t):
    return pltpu.roll(t, RANK, 1)


def kernel(
    ZN, XN, YN,
    signal, near_hbm, near_block, basis, far0_hbm, coupling0, transfer1, transfer2,
    far1_index, coupling1, far2_index, coupling2,
    first, second,
    fld, xs, hf, na, ah, al, bs, bh, bl, wh, wl, sh, sl, t1, t2, c0, c0h, c0l,
    c1s, c2s, c1f, c1h, c1l, c2f, c2h, c2l,
    yb, cba, cbb, gba, gbb, psx, pbx, psz, pbz, lcs, lch, lcd, acc, near_index, far0_index, si1, si2,
    in_sem, sig_sem, near_sem, out_sem, hs, hr, es, er, ys, yr, zs, zr, gs, gr, fs, fr,
    pxs, pxr, pzs, pzr, k1s, k1r, k2s, k2r, i1s, i1r, i2s, i2r,
):
    leaf = lax.axis_index("leaf")
    y = lax.axis_index("grp")
    c = lax.rem(leaf, 2)
    x = lax.rem(leaf // 2, XN)
    z = leaf // (2 * XN)
    leaves = 2 * XN * ZN
    cb, gb = (cba, cbb), (gba, gbb)
    low = lax.broadcasted_iota(jnp.int32, (RHS, LANES), 1) < RANK
    low_half = lax.broadcasted_iota(jnp.int32, (PACK, LANES), 1) < RANK
    half = LEAF // 2

    def at(zz, xx, cc, yy):
        return ((zz * XN + xx) * 2 + cc, yy)

    y_peers = [lax.rem(y + o, YN) for o in range(1, YN)]
    x_peers = [lax.rem(x + o, XN) for o in range(1, XN)]
    z_peers = [lax.rem(z + o, ZN) for o in range(1, ZN)]
    sibling = at(z, x, 1 - c, y)
    after = (lax.rem(leaf + (y + 1) // YN, leaves), lax.rem(y + 1, YN))
    before = (lax.rem(leaf + leaves - 1 + (y + YN - 1) // YN, leaves), lax.rem(y + YN - 1, YN))

    def remote(src, dst, ssem, rsem, dev):
        return pltpu.make_async_remote_copy(
            src_ref=src, dst_ref=dst, send_sem=ssem, recv_sem=rsem, device_id=dev, device_id_type=MESH
        )

    def pack(v):
        w = jnp.concatenate([v, jnp.zeros_like(v)], axis=1)
        return w[:PACK] + swap(w[PACK:])

    def pack_low(t):
        return jnp.where(low_half, t[:PACK], swap(t[PACK:]))

    def pack_high(t):
        return jnp.where(low_half, swap(t[:PACK]), t[PACK:])

    def pair_of(a, b):
        return jnp.where(
            low, jnp.concatenate([a, swap(a)], axis=0), jnp.concatenate([swap(b), b], axis=0)
        )

    def signal_load(i):
        return pltpu.make_async_copy(signal.at[:, pl.ds(i * NODE, NODE)], fld.at[0, i], sig_sem.at[i])

    def near_load(l):
        return pltpu.make_async_copy(near_block.at[l], na.at[l], near_sem.at[l])

    loads = []
    for n, (src, dst) in enumerate((
        (basis, bs), (transfer1, t1), (transfer2.at[0], t2),
        (far1_index, si1.at[x]), (far2_index, si2.at[z]), (coupling1.at[0], c1s), (coupling2.at[0], c2s),
        (coupling0, c0), (near_hbm, near_index), (far0_hbm, far0_index),
    )):
        loads.append(pltpu.make_async_copy(src, dst, in_sem.at[n]))
    for i in range(LEAF):
        signal_load(i).start()
    for cp in loads:
        cp.start()
    for l in range(LEAF):
        near_load(l).start()

    greet = [at(z, x, c, yy) for yy in y_peers] + [at(z, xx, c, y) for xx in x_peers]
    greet += [at(zz, x, c, y) for zz in z_peers] + [sibling, after, before]
    barrier = pltpu.get_barrier_semaphore()
    for dev in greet:
        pl.semaphore_signal(barrier, inc=1, device_id=dev, device_id_type=MESH)

    def halo(p, side, i):
        return remote(
            fld.at[p, i], hf.at[p, side, i], hs.at[p, side, i], hr.at[p, side, i], after if side == 0 else before
        )

    def send_halo(p):
        for i in range(LEAF):
            halo(p, 0, LEAF - 1 - i).start()
            halo(p, 1, i).start()

    def coupling_copies():
        out = [
            (remote(c1f.at[x], c1f.at[x], k1s.at[xx], k1r.at[x], at(z, xx, c, y)),
             remote(si1.at[x], si1.at[x], i1s.at[xx], i1r.at[x], at(z, xx, c, y)))
            for xx in x_peers
        ]
        out += [
            (remote(c2f.at[z], c2f.at[z], k2s.at[zz], k2r.at[z], at(zz, x, c, y)),
             remote(si2.at[z], si2.at[z], i2s.at[zz], i2r.at[z], at(zz, x, c, y)))
            for zz in z_peers
        ]
        return out

    base = (leaf * YN + y) * LEAF - LEAF

    def near_split(l, carry):
        near_load(l).wait()
        for k in range(NEAR):
            ah[l, k], al[l, k] = split(na[l, k])
        return carry

    def near_own(l, carry):
        acc[l] = product(dot_nt, xs[LEAF + l], ah[l, 0], al[l, 0])
        return carry

    def coupling_split(l, carry):
        for j in range(FAR // 2):
            hi, lo = split(jnp.concatenate([c0[l, 2 * j], c0[l, 2 * j + 1]], axis=1))
            c0h[l, :, pl.ds(j * LANES, LANES)] = hi
            c0l[l, :, pl.ds(j * LANES, LANES)] = lo
        return carry

    def coef_copy(p, side):
        return remote(lcs.at[p], lch.at[p, side], es.at[p, side], er.at[p, side], after if side == 0 else before)

    def y_copy(p, yy, slot):
        return remote(yb.at[p, slot], yb.at[p, slot], ys.at[p, yy], yr.at[p, slot], at(z, x, c, yy))

    def z_copy(p, zz, slot):
        return remote(cb[p].at[0, slot], cb[p].at[0, slot], zs.at[p, zz], zr.at[p, slot], at(zz, x, c, y))

    def g_copy(p, xx, slot):
        return remote(gb[p].at[0, slot], gb[p].at[0, slot], gs.at[p, xx], gr.at[p, slot], at(z, xx, c, y))

    def forward(p):
        return (
            remote(cb[p].at[0], cb[p].at[1], fs.at[p, 0], fr.at[p, 0], sibling),
            remote(gb[p].at[0], gb[p].at[1], fs.at[p, 1], fr.at[p, 1], sibling),
        )

    def px_copy(p, xx, slot):
        return remote(psx.at[p, xx], pbx.at[p, slot], pxs.at[p, xx], pxr.at[p, slot], at(z, xx, c, y))

    def pz_copy(p, zz, slot):
        return remote(psz.at[p, zz], pbz.at[p, slot], pzs.at[p, zz], pzr.at[p, slot], at(zz, x, c, y))

    def wide(i):
        return jnp.minimum(jnp.maximum(i - base, 0), 3 * LEAF - 1)

    def slot_of(cc):
        return jnp.where(cc == c, 0, 1)

    def mid_tile(p, m, k):
        i = si1[m, 0, k]
        g = lax.div(i, YN)
        h = lax.div(g, 2)
        t = cb[p][slot_of(lax.rem(g, 2)), lax.div(h, XN), lax.rem(i, YN)]
        return jnp.where(lax.rem(h, XN) == x, t, 0.0)

    def top_tile(p, m, k):
        i = si2[m, 0, k]
        h = lax.div(i, 2)
        t = gb[p][slot_of(lax.rem(i, 2)), lax.rem(h, XN)]
        return jnp.where(lax.div(h, XN) == z, t, 0.0)

    def leaf_tile(l, k):
        return lcd[wide(far0_index[l, k])]

    def picked(pair):
        return jnp.concatenate([stacked(pair(j)) for j in range(FAR // 2)], axis=1)

    def coefs(p):
        for j in range(half):
            pair = jnp.concatenate(
                [product(dot_nt, xs[LEAF + l], bh[l], bl[l]) for l in (2 * j, 2 * j + 1)], axis=1
            )
            other = swap(pair)
            lcs[p, j] = pair
            lcd[LEAF + 2 * j] = jnp.where(low, pair, other)
            lcd[LEAF + 2 * j + 1] = jnp.where(low, other, pair)

    def send_up(p, u):
        yb[p, y, 0] = pack_low(u)
        yb[p, y, 1] = pack_high(u)
        for yy in y_peers:
            y_copy(p, yy, y).start()

    def group(p):
        for yy in y_peers:
            y_copy(p, yy, yy).wait_recv()
        total = yb[p, 0, 1]
        for i in range(1, YN):
            total = total + yb[p, i, 1]
        gb[p][0, x] = total
        for xx in x_peers:
            g_copy(p, xx, x).start()
        for i in range(YN):
            cb[p][0, z, i] = yb[p, i, 0]
        for zz in z_peers:
            z_copy(p, zz, z).start()

    def far_leaves(p):
        for side in range(2):
            coef_copy(p, side).wait_recv()
        for j in range(half):
            for side in range(2):
                t = lch[p, side, j]
                r = swap(t)
                lcd[side * 2 * LEAF + 2 * j] = jnp.where(low, t, r)
                lcd[side * 2 * LEAF + 2 * j + 1] = jnp.where(low, r, t)

        for l in range(LEAF):
            v = picked(lambda j: jnp.where(low, leaf_tile(l, 2 * j), leaf_tile(l, 2 * j + 1)))
            v = product(dot_nt, v, c0h[l], c0l[l])
            acc[l] += product(dot_nn, stacked(v), bh[l], bl[l])

    def send_forward(p):
        for zz in z_peers:
            z_copy(p, zz, zz).wait_recv()
        for xx in x_peers:
            g_copy(p, xx, xx).wait_recv()
        for cp in forward(p):
            cp.start()

    def partials(p):
        for cp in forward(p):
            cp.wait_recv()
        for m in range(XN):
            v = picked(lambda j: pair_of(mid_tile(p, m, 2 * j), mid_tile(p, m, 2 * j + 1)))
            psx[p, m] = pack(product(dot_nt, v, c1h[m], c1l[m]))
        for xx in x_peers:
            px_copy(p, xx, x).start()
        for m in range(ZN):
            v = picked(lambda j: pair_of(top_tile(p, m, 2 * j), top_tile(p, m, 2 * j + 1)))
            psz[p, m] = pack(product(dot_nt, v, c2h[m], c2l[m]))
        for zz in z_peers:
            pz_copy(p, zz, z).start()

    def near(p):
        def take(side, i):
            halo(p, side, i).wait_recv()
            xs[side * 2 * LEAF + i] = stacked(hf[p, side, i])

        def near_leaf(l):
            total = acc[l]
            for k in range(1, NEAR):
                total = total + product(dot_nt, xs[wide(near_index[k, l])], ah[l, k], al[l, k])
            acc[l] = total

        def take_first(i, carry):
            take(0, LEAF - 1 - i)
            take(1, i)
            return carry

        lax.fori_loop(0, half, take_first, 0)

        def near_pair(j, carry):
            take(0, half - 1 - j)
            take(1, half + j)
            near_leaf(half - 1 - j)
            near_leaf(half + j)
            return carry

        lax.fori_loop(0, half, near_pair, 0)

    def from_above(p):
        for xx in x_peers:
            px_copy(p, xx, xx).wait_recv()
        for zz in z_peers:
            pz_copy(p, zz, zz).wait_recv()
        mid = psx[p, x]
        for xx in x_peers:
            mid = mid + pbx[p, xx]
        top = psz[p, z]
        for zz in z_peers:
            top = top + pbz[p, zz]
        return stacked(pair_of(mid, top))

    def write(p, l):
        out = first if p == 0 else second
        return pltpu.make_async_copy(fld.at[p + 1, l], out.at[:, pl.ds(l * NODE, NODE)], out_sem.at[p, l])

    def finish(p, down):
        for l in range(LEAF):
            v = acc[l] + product(dot_nn, down, wh[l], wl[l])
            fld[p + 1, l] = v
            if p == 0:
                xs[LEAF + l] = stacked(v)
        for l in range(LEAF):
            write(p, l).start()

    for i in range(LEAF):
        signal_load(i).wait()
    for cp in loads[:3]:
        cp.wait()
    for l in range(LEAF):
        bh[l], bl[l] = split(bs[l])
        xs[LEAF + l] = stacked(fld[0, l])
    coefs(0)
    t1p = split(t1[...].reshape(WIDE, RANK))
    t2p = split(t2[...])
    low_level = jnp.concatenate([stacked(lcs[0, j]) for j in range(half)], axis=1)
    cluster = product(dot_nn, low_level, *t1p)
    up = jnp.concatenate([cluster, product(dot_nn, stacked(cluster), *t2p)], axis=1)

    pl.semaphore_wait(barrier, len(greet))
    send_up(0, up)
    for side in range(2):
        coef_copy(0, side).start()
    for cp in loads[3:7]:
        cp.wait()
    for j in range(FAR // 2):
        c1f[x, :, pl.ds(j * LANES, LANES)] = jnp.concatenate([c1s[2 * j], c1s[2 * j + 1]], axis=1)
        c2f[z, :, pl.ds(j * LANES, LANES)] = jnp.concatenate([c2s[2 * j], c2s[2 * j + 1]], axis=1)
    for pair in coupling_copies():
        for cp in pair:
            cp.start()
    send_halo(0)

    for l in range(LEAF):
        xs[l] = jnp.zeros((2 * RHS, NODE), BF16)
        xs[2 * LEAF + l] = jnp.zeros((2 * RHS, NODE), BF16)
    lax.fori_loop(0, LEAF, near_split, 0)
    group(0)

    t1a, t1b = split(t1[...].reshape(WIDE, RANK))
    t12 = three(dot_nn, (t1a, t1b), split(t2[...]))
    for l in range(LEAF):
        e = split(jnp.concatenate([t1[l], t12[l * RANK:(l + 1) * RANK]], axis=1))
        wh[l], wl[l] = split(three(dot_tn, e, (bh[l], bl[l])))
    for cp in loads[7:]:
        cp.wait()
    lax.fori_loop(0, LEAF, coupling_split, 0)
    lax.fori_loop(0, LEAF, near_own, 0)
    send_forward(0)
    square = three(dot_nt, (wh[0], wl[0]), (wh[0], wl[0]))
    for l in range(1, LEAF):
        square = square + three(dot_nt, (wh[l], wl[l]), (wh[l], wl[l]))
    sh[...], sl[...] = split(square)
    far_leaves(0)
    for xx in x_peers:
        remote(c1f.at[xx], c1f.at[xx], k1s.at[xx], k1r.at[xx], at(z, xx, c, y)).wait_recv()
        remote(si1.at[xx], si1.at[xx], i1s.at[xx], i1r.at[xx], at(z, xx, c, y)).wait_recv()
    for zz in z_peers:
        remote(c2f.at[zz], c2f.at[zz], k2s.at[zz], k2r.at[zz], at(zz, x, c, y)).wait_recv()
        remote(si2.at[zz], si2.at[zz], i2s.at[zz], i2r.at[zz], at(zz, x, c, y)).wait_recv()
    for m in range(XN):
        c1h[m], c1l[m] = split(c1f[m])
    for m in range(ZN):
        c2h[m], c2l[m] = split(c2f[m])
    partials(0)
    near(0)
    up = product(dot_nt, stacked(acc[0]), wh[0], wl[0])
    for l in range(1, LEAF):
        up = up + product(dot_nt, stacked(acc[l]), wh[l], wl[l])
    down = from_above(0)

    send_up(1, up + product(dot_nn, down, sh[...], sl[...]))
    finish(0, down)
    coefs(1)
    for side in range(2):
        coef_copy(1, side).start()
    send_halo(1)
    lax.fori_loop(0, LEAF, near_own, 0)
    group(1)
    far_leaves(1)
    send_forward(1)
    partials(1)
    near(1)
    finish(1, from_above(1))

    for pair in coupling_copies():
        for cp in pair:
            cp.wait_send()
    for p in range(2):
        for side in range(2):
            for i in range(LEAF):
                halo(p, side, i).wait_send()
            coef_copy(p, side).wait_send()
        for yy in y_peers:
            y_copy(p, yy, y).wait_send()
        for zz in z_peers:
            z_copy(p, zz, z).wait_send()
            pz_copy(p, zz, z).wait_send()
        for xx in x_peers:
            g_copy(p, xx, x).wait_send()
            px_copy(p, xx, x).wait_send()
        for cp in forward(p):
            cp.wait_send()
        for l in range(LEAF):
            write(p, l).wait()


def hand_over(a, b, first, second, sem):
    copies = [pltpu.make_async_copy(a, first, sem.at[0]), pltpu.make_async_copy(b, second, sem.at[1])]
    for cp in copies:
        cp.start()
    for cp in copies:
        cp.wait()


def solution(mesh):
    leaf, grp = ("leaf", "grp")
    YN = mesh.shape[grp]
    XN = ZN = math.isqrt(mesh.shape[leaf] // 2)
    both = (leaf, grp)
    placed = (
        P(None, both),
        P(both, None),
        P(both, None, None, None),
        P(both, None, None),
        P(both, None),
        P(both, None, None, None),
        P(both, None, None),
        P(both, None, None),
        P(both, None),
        P(both, None, None, None),
        P(leaf, None),
        P(leaf, None, None, None),
    )

    def body(*refs):
        return kernel(ZN, XN, YN, *refs)

    hbm = pl.BlockSpec(memory_space=pl.ANY)
    anywhere = pl.BlockSpec(memory_space=pl.ANY)
    vmem = pltpu.VMEM
    dma = pltpu.SemaphoreType.DMA
    cols = LEAF * NODE
    scratch = [
        vmem((3, LEAF, RHS, NODE), F32),
        vmem((3 * LEAF, 2 * RHS, NODE), BF16),
        vmem((2, 2, LEAF, RHS, NODE), F32),
        vmem((LEAF, NEAR, NODE, NODE), F32),
        vmem((LEAF, NEAR, NODE, NODE), BF16),
        vmem((LEAF, NEAR, NODE, NODE), BF16),
        vmem((LEAF, RANK, NODE), F32),
        vmem((LEAF, RANK, NODE), BF16),
        vmem((LEAF, RANK, NODE), BF16),
        vmem((LEAF, LANES, NODE), BF16),
        vmem((LEAF, LANES, NODE), BF16),
        vmem((LANES, LANES), BF16),
        vmem((LANES, LANES), BF16),
        vmem((LEAF, RANK, RANK), F32),
        vmem((RANK, RANK), F32),
        vmem((LEAF, FAR, RANK, RANK), F32),
        vmem((LEAF, RANK, WIDE), BF16),
        vmem((LEAF, RANK, WIDE), BF16),
        vmem((FAR, RANK, RANK), F32),
        vmem((FAR, RANK, RANK), F32),
        vmem((XN, RANK, WIDE), F32),
        vmem((XN, RANK, WIDE), BF16),
        vmem((XN, RANK, WIDE), BF16),
        vmem((ZN, RANK, WIDE), F32),
        vmem((ZN, RANK, WIDE), BF16),
        vmem((ZN, RANK, WIDE), BF16),
        vmem((2, YN, 2, PACK, LANES), F32),
        vmem((2, ZN, YN, PACK, LANES), F32),
        vmem((2, ZN, YN, PACK, LANES), F32),
        vmem((2, XN, PACK, LANES), F32),
        vmem((2, XN, PACK, LANES), F32),
        vmem((2, XN, PACK, LANES), F32),
        vmem((2, XN, PACK, LANES), F32),
        vmem((2, ZN, PACK, LANES), F32),
        vmem((2, ZN, PACK, LANES), F32),
        vmem((2, LEAF // 2, RHS, 2 * RANK), F32),
        vmem((2, 2, LEAF // 2, RHS, 2 * RANK), F32),
        vmem((3 * LEAF, RHS, 2 * RANK), F32),
        vmem((LEAF, RHS, NODE), F32),
        pltpu.SMEM((NEAR, LEAF), jnp.int32),
        pltpu.SMEM((LEAF, FAR), jnp.int32),
        pltpu.SMEM((XN, 1, FAR), jnp.int32),
        pltpu.SMEM((ZN, 1, FAR), jnp.int32),
        dma((10,)), dma((LEAF,)), dma((LEAF,)), dma((2, LEAF)),
        dma((2, 2, LEAF)), dma((2, 2, LEAF)),
        dma((2, 2)), dma((2, 2)),
        dma((2, YN)), dma((2, YN)),
        dma((2, ZN)), dma((2, ZN)),
        dma((2, XN)), dma((2, XN)),
        dma((2, 2)), dma((2, 2)),
        dma((2, XN)), dma((2, XN)),
        dma((2, ZN)), dma((2, ZN)),
        dma((XN,)), dma((XN,)), dma((ZN,)), dma((ZN,)),
        dma((XN,)), dma((XN,)), dma((ZN,)), dma((ZN,)),
    ]

    def per_device(signal, near_index, near_block, basis, *rest):
        args = (signal, near_index.T, near_block, jnp.swapaxes(basis, 1, 2), *rest)
        call = pl.pallas_call(
            body,
            out_shape=[jax.ShapeDtypeStruct((RHS, cols), F32)] * 2,
            in_specs=[hbm] * 12,
            out_specs=[anywhere, anywhere],
            scratch_shapes=scratch,
            compiler_params=pltpu.CompilerParams(
                collective_id=0, has_side_effects=True, vmem_limit_bytes=56 * 1024 * 1024
            ),
        )
        images = call(*args)
        final = pl.pallas_call(
            hand_over,
            out_shape=[jax.ShapeDtypeStruct((RHS, cols), F32)] * 2,
            in_specs=[pl.BlockSpec(memory_space=vmem)] * 2,
            out_specs=[hbm, hbm],
            scratch_shapes=[dma((2,))],
        )
        return tuple(final(*images))

    return jax.shard_map(
        per_device,
        mesh=mesh,
        in_specs=placed,
        out_specs=(P(None, both), P(None, both)),
        check_vma=False,
    )
```

```python
import math

import jax
import jax.numpy as jnp
from jax import lax
from jax.experimental import pallas as pl
from jax.experimental.pallas import tpu as pltpu
from jax.sharding import PartitionSpec as P

F32 = jnp.float32
BF16 = jnp.bfloat16
MESH = pl.DeviceIdType.MESH
LEAF = 8
NODE = 256
RANK = 64
RHS = 32
NEAR = 4
FAR = 8
WIDE = RANK * FAR
PACK = RHS // 2
LANES = 2 * RANK


def dot(a, b, da, db):
    return lax.dot_general(a, b, (((da,), (db,)), ((), ())), preferred_element_type=F32)


def dot_nt(a, b):
    return dot(a, b, 1, 1)


def dot_nn(a, b):
    return dot(a, b, 1, 0)


def dot_tn(a, b):
    return dot(a, b, 0, 0)


def split(t):
    hi = t.astype(BF16)
    return hi, (t - hi.astype(F32)).astype(BF16)


def stacked(t):
    return jnp.concatenate(split(t), axis=0)


def product(f, x, wh, wl):
    r = f(x, wh)
    return r[:RHS] + r[RHS:] + f(x[:RHS], wl)


def three(f, a, b):
    return f(a[0], b[0]) + f(a[1], b[0]) + f(a[0], b[1])


def swap(t):
    return pltpu.roll(t, RANK, 1)


def kernel(
    ZN, XN, YN,
    signal, near_hbm, near_block, basis, far0_hbm, coupling0, transfer1, transfer2,
    far1_index, coupling1, far2_index, coupling2,
    first, second,
    fld, xs, hf, na, ah, al, bs, bh, bl, wh, wl, sh, sl, t1, t2, c0, c0h, c0l,
    c1s, c2s, c1f, c1h, c1l, c2f, c2h, c2l,
    yb, lb, cba, cbb, gba, gbb, psx, pbx, psz, pbz, lcs, lch, lcd, acc, near_index, far0_index, si1, si2,
    in_sem, sig_sem, near_sem, out_sem, hs, hr, es, er, ys, yr, zs, zr, gs, gr, fs, fr, fgs, fgr,
    pxs, pxr, pzs, pzr, k1s, k1r, k2s, k2r, i1s, i1r, i2s, i2r,
):
    leaf = lax.axis_index("leaf")
    y = lax.axis_index("grp")
    c = lax.rem(leaf, 2)
    x = lax.rem(leaf // 2, XN)
    z = leaf // (2 * XN)
    leaves = 2 * XN * ZN
    cb, gb = (cba, cbb), (gba, gbb)
    low = lax.broadcasted_iota(jnp.int32, (RHS, LANES), 1) < RANK
    low_half = lax.broadcasted_iota(jnp.int32, (PACK, LANES), 1) < RANK
    half = LEAF // 2

    def at(zz, xx, cc, yy):
        return ((zz * XN + xx) * 2 + cc, yy)

    y_peers = [lax.rem(y + o, YN) for o in range(1, YN)]
    x_peers = [lax.rem(x + o, XN) for o in range(1, XN)]
    z_peers = [lax.rem(z + o, ZN) for o in range(1, ZN)]
    sibling = at(z, x, 1 - c, y)
    after = (lax.rem(leaf + (y + 1) // YN, leaves), lax.rem(y + 1, YN))
    before = (lax.rem(leaf + leaves - 1 + (y + YN - 1) // YN, leaves), lax.rem(y + YN - 1, YN))

    def remote(src, dst, ssem, rsem, dev):
        return pltpu.make_async_remote_copy(
            src_ref=src, dst_ref=dst, send_sem=ssem, recv_sem=rsem, device_id=dev, device_id_type=MESH
        )

    def pack(v):
        w = jnp.concatenate([v, jnp.zeros_like(v)], axis=1)
        return w[:PACK] + swap(w[PACK:])

    def pack_low(t):
        return jnp.where(low_half, t[:PACK], swap(t[PACK:]))

    def pack_high(t):
        return jnp.where(low_half, swap(t[:PACK]), t[PACK:])

    def pair_of(a, b):
        return jnp.where(
            low, jnp.concatenate([a, swap(a)], axis=0), jnp.concatenate([swap(b), b], axis=0)
        )

    def signal_load(i):
        return pltpu.make_async_copy(signal.at[:, pl.ds(i * NODE, NODE)], fld.at[0, i], sig_sem.at[i])

    def near_load(l):
        return pltpu.make_async_copy(near_block.at[l], na.at[l], near_sem.at[l])

    loads = []
    for n, (src, dst) in enumerate((
        (basis, bs), (transfer1, t1), (transfer2.at[0], t2),
        (far1_index, si1.at[x]), (far2_index, si2.at[z]), (coupling1.at[0], c1s), (coupling2.at[0], c2s),
        (coupling0, c0), (near_hbm, near_index), (far0_hbm, far0_index),
    )):
        loads.append(pltpu.make_async_copy(src, dst, in_sem.at[n]))
    for i in range(LEAF):
        signal_load(i).start()
    for cp in loads:
        cp.start()
    for l in range(LEAF):
        near_load(l).start()

    every_y = [lax.rem(y + o, YN) for o in range(YN)]
    greet = [at(z, x, c, yy) for yy in y_peers] + [at(z, xx, c, yy) for xx in x_peers for yy in every_y]
    greet += [at(zz, x, c, yy) for zz in z_peers for yy in every_y] + [sibling, after, before]
    barrier = pltpu.get_barrier_semaphore()
    for dev in greet:
        pl.semaphore_signal(barrier, inc=1, device_id=dev, device_id_type=MESH)

    def halo(p, side, i):
        return remote(
            fld.at[p, i], hf.at[p, side, i], hs.at[p, side, i], hr.at[p, side, i], after if side == 0 else before
        )

    def send_halo(p):
        for i in range(LEAF):
            halo(p, 0, LEAF - 1 - i).start()
            halo(p, 1, i).start()

    def coupling_copies():
        out = [
            (remote(c1f.at[x], c1f.at[x], k1s.at[xx], k1r.at[x], at(z, xx, c, y)),
             remote(si1.at[x], si1.at[x], i1s.at[xx], i1r.at[x], at(z, xx, c, y)))
            for xx in x_peers
        ]
        out += [
            (remote(c2f.at[z], c2f.at[z], k2s.at[zz], k2r.at[z], at(zz, x, c, y)),
             remote(si2.at[z], si2.at[z], i2s.at[zz], i2r.at[z], at(zz, x, c, y)))
            for zz in z_peers
        ]
        return out

    base = (leaf * YN + y) * LEAF - LEAF

    def near_split(l, carry):
        near_load(l).wait()
        for k in range(NEAR):
            ah[l, k], al[l, k] = split(na[l, k])
        return carry

    def near_own():
        for l in range(LEAF):
            acc[l] = product(dot_nt, xs[LEAF + l], ah[l, 0], al[l, 0])

    def coupling_split(l, carry):
        for j in range(FAR // 2):
            hi, lo = split(jnp.concatenate([c0[l, 2 * j], c0[l, 2 * j + 1]], axis=1))
            c0h[l, :, pl.ds(j * LANES, LANES)] = hi
            c0l[l, :, pl.ds(j * LANES, LANES)] = lo
        return carry

    def coef_copy(p, side):
        return remote(lcs.at[p], lch.at[p, side], es.at[p, side], er.at[p, side], after if side == 0 else before)

    def y_copy(p, yy, slot):
        return remote(yb.at[p, slot], yb.at[p, slot], ys.at[p, yy], yr.at[p, slot], at(z, x, c, yy))

    def z_copy(p, zz, yy, slot_z, slot_y):
        return remote(
            yb.at[p, y, 0], cb[p].at[0, slot_z, slot_y], zs.at[p, zz, yy], zr.at[p, slot_z, slot_y], at(zz, x, c, yy)
        )

    def g_copy(p, xx, yy, slot_x, slot_y):
        return remote(
            yb.at[p, y, 1], lb.at[p, slot_x, slot_y], gs.at[p, xx, yy], gr.at[p, slot_x, slot_y], at(z, xx, c, yy)
        )

    def forward(p, zz):
        return remote(cb[p].at[0, zz], cb[p].at[1, zz], fs.at[p, zz], fr.at[p, zz], sibling)

    def forward_top(p):
        return remote(gb[p].at[0], gb[p].at[1], fgs.at[p], fgr.at[p], sibling)

    def px_copy(p, xx, slot):
        return remote(psx.at[p, xx], pbx.at[p, slot], pxs.at[p, xx], pxr.at[p, slot], at(z, xx, c, y))

    def pz_copy(p, zz, slot):
        return remote(psz.at[p, zz], pbz.at[p, slot], pzs.at[p, zz], pzr.at[p, slot], at(zz, x, c, y))

    def wide(i):
        return jnp.minimum(jnp.maximum(i - base, 0), 3 * LEAF - 1)

    def slot_of(cc):
        return jnp.where(cc == c, 0, 1)

    def mid_tile(p, m, k):
        i = si1[m, 0, k]
        g = lax.div(i, YN)
        h = lax.div(g, 2)
        t = cb[p][slot_of(lax.rem(g, 2)), lax.div(h, XN), lax.rem(i, YN)]
        return jnp.where(lax.rem(h, XN) == x, t, 0.0)

    def top_tile(p, m, k):
        i = si2[m, 0, k]
        h = lax.div(i, 2)
        t = gb[p][slot_of(lax.rem(i, 2)), lax.rem(h, XN)]
        return jnp.where(lax.div(h, XN) == z, t, 0.0)

    def leaf_tile(l, k):
        return lcd[wide(far0_index[l, k])]

    def picked(pair):
        return jnp.concatenate([stacked(pair(j)) for j in range(FAR // 2)], axis=1)

    def coefs(p):
        for j in range(half):
            pair = jnp.concatenate(
                [product(dot_nt, xs[LEAF + l], bh[l], bl[l]) for l in (2 * j, 2 * j + 1)], axis=1
            )
            other = swap(pair)
            lcs[p, j] = pair
            lcd[LEAF + 2 * j] = jnp.where(low, pair, other)
            lcd[LEAF + 2 * j + 1] = jnp.where(low, other, pair)

    def send_up(p, u):
        yb[p, y, 0] = pack_low(u)
        yb[p, y, 1] = pack_high(u)
        for xx, zz in zip(x_peers, z_peers):
            for yy in every_y[1:] + every_y[:1]:
                g_copy(p, xx, yy, x, y).start()
                z_copy(p, zz, yy, z, y).start()
        for yy in y_peers:
            y_copy(p, yy, y).start()

    def group(p):
        for yy in y_peers:
            y_copy(p, yy, yy).wait_recv()
        total = yb[p, 0, 1]
        for i in range(1, YN):
            total = total + yb[p, i, 1]
        gb[p][0, x] = total
        for i in range(YN):
            cb[p][0, z, i] = yb[p, i, 0]
        forward(p, z).start()
        for xx in x_peers:
            for yy in every_y:
                g_copy(p, xx, yy, xx, yy).wait_recv()
            total = lb[p, xx, 0]
            for i in range(1, YN):
                total = total + lb[p, xx, i]
            gb[p][0, xx] = total
        forward_top(p).start()
        for zz in z_peers:
            for yy in every_y:
                z_copy(p, zz, yy, zz, yy).wait_recv()
            forward(p, zz).start()

    def far_leaves(p):
        for side in range(2):
            coef_copy(p, side).wait_recv()
        for j in range(half):
            for side in range(2):
                t = lch[p, side, j]
                r = swap(t)
                lcd[side * 2 * LEAF + 2 * j] = jnp.where(low, t, r)
                lcd[side * 2 * LEAF + 2 * j + 1] = jnp.where(low, r, t)

        tiles = [
            picked(lambda j: jnp.where(low, leaf_tile(l, 2 * j), leaf_tile(l, 2 * j + 1))) for l in range(LEAF)
        ]
        sums = [stacked(product(dot_nt, tiles[l], c0h[l], c0l[l])) for l in range(LEAF)]
        for l in range(LEAF):
            acc[l] += product(dot_nn, sums[l], bh[l], bl[l])

    def partials(p):
        for zz in [z] + z_peers:
            forward(p, zz).wait_recv()
        forward_top(p).wait_recv()
        for m in range(XN):
            v = picked(lambda j: pair_of(mid_tile(p, m, 2 * j), mid_tile(p, m, 2 * j + 1)))
            psx[p, m] = pack(product(dot_nt, v, c1h[m], c1l[m]))
        for xx in x_peers:
            px_copy(p, xx, x).start()
        for m in range(ZN):
            v = picked(lambda j: pair_of(top_tile(p, m, 2 * j), top_tile(p, m, 2 * j + 1)))
            psz[p, m] = pack(product(dot_nt, v, c2h[m], c2l[m]))
        for zz in z_peers:
            pz_copy(p, zz, z).start()

    def near(p):
        def take(side, i):
            halo(p, side, i).wait_recv()
            xs[side * 2 * LEAF + i] = stacked(hf[p, side, i])

        def near_leaf(l):
            total = acc[l]
            for k in range(1, NEAR):
                total = total + product(dot_nt, xs[wide(near_index[k, l])], ah[l, k], al[l, k])
            acc[l] = total

        def take_first(i, carry):
            take(0, LEAF - 1 - i)
            take(1, i)
            return carry

        lax.fori_loop(0, half, take_first, 0)

        def near_pair(j, carry):
            take(0, half - 1 - j)
            take(1, half + j)
            near_leaf(half - 1 - j)
            near_leaf(half + j)
            return carry

        lax.fori_loop(0, half, near_pair, 0)

    def from_above(p):
        for xx in x_peers:
            px_copy(p, xx, xx).wait_recv()
        for zz in z_peers:
            pz_copy(p, zz, zz).wait_recv()
        mid = psx[p, x]
        for xx in x_peers:
            mid = mid + pbx[p, xx]
        top = psz[p, z]
        for zz in z_peers:
            top = top + pbz[p, zz]
        return stacked(pair_of(mid, top))

    def write(p, l):
        out = first if p == 0 else second
        return pltpu.make_async_copy(fld.at[p + 1, l], out.at[:, pl.ds(l * NODE, NODE)], out_sem.at[p, l])

    def finish(p, down):
        for l in range(LEAF):
            v = acc[l] + product(dot_nn, down, wh[l], wl[l])
            fld[p + 1, l] = v
            if p == 0:
                xs[LEAF + l] = stacked(v)
        for l in range(LEAF):
            write(p, l).start()

    for i in range(LEAF):
        signal_load(i).wait()
    for cp in loads[:3]:
        cp.wait()
    for l in range(LEAF):
        bh[l], bl[l] = split(bs[l])
        xs[LEAF + l] = stacked(fld[0, l])
    coefs(0)
    t1p = split(t1[...].reshape(WIDE, RANK))
    t2p = split(t2[...])
    low_level = jnp.concatenate([stacked(lcs[0, j]) for j in range(half)], axis=1)
    cluster = product(dot_nn, low_level, *t1p)
    up = jnp.concatenate([cluster, product(dot_nn, stacked(cluster), *t2p)], axis=1)

    pl.semaphore_wait(barrier, len(greet))
    send_up(0, up)
    for side in range(2):
        coef_copy(0, side).start()
    for cp in loads[3:7]:
        cp.wait()
    for j in range(FAR // 2):
        c1f[x, :, pl.ds(j * LANES, LANES)] = jnp.concatenate([c1s[2 * j], c1s[2 * j + 1]], axis=1)
        c2f[z, :, pl.ds(j * LANES, LANES)] = jnp.concatenate([c2s[2 * j], c2s[2 * j + 1]], axis=1)
    for pair in coupling_copies():
        for cp in pair:
            cp.start()
    send_halo(0)

    for l in range(LEAF):
        xs[l] = jnp.zeros((2 * RHS, NODE), BF16)
        xs[2 * LEAF + l] = jnp.zeros((2 * RHS, NODE), BF16)
    lax.fori_loop(0, LEAF, near_split, 0)
    group(0)

    t1a, t1b = split(t1[...].reshape(WIDE, RANK))
    t12 = three(dot_nn, (t1a, t1b), split(t2[...]))
    for l in range(LEAF):
        e = split(jnp.concatenate([t1[l], t12[l * RANK:(l + 1) * RANK]], axis=1))
        wh[l], wl[l] = split(three(dot_tn, e, (bh[l], bl[l])))
    for cp in loads[7:]:
        cp.wait()
    lax.fori_loop(0, LEAF, coupling_split, 0)
    near_own()
    square = three(dot_nt, (wh[0], wl[0]), (wh[0], wl[0]))
    for l in range(1, LEAF):
        square = square + three(dot_nt, (wh[l], wl[l]), (wh[l], wl[l]))
    sh[...], sl[...] = split(square)
    far_leaves(0)
    for xx in x_peers:
        remote(c1f.at[xx], c1f.at[xx], k1s.at[xx], k1r.at[xx], at(z, xx, c, y)).wait_recv()
        remote(si1.at[xx], si1.at[xx], i1s.at[xx], i1r.at[xx], at(z, xx, c, y)).wait_recv()
    for zz in z_peers:
        remote(c2f.at[zz], c2f.at[zz], k2s.at[zz], k2r.at[zz], at(zz, x, c, y)).wait_recv()
        remote(si2.at[zz], si2.at[zz], i2s.at[zz], i2r.at[zz], at(zz, x, c, y)).wait_recv()
    for m in range(XN):
        c1h[m], c1l[m] = split(c1f[m])
    for m in range(ZN):
        c2h[m], c2l[m] = split(c2f[m])
    partials(0)
    near(0)
    up = product(dot_nt, stacked(acc[0]), wh[0], wl[0])
    for l in range(1, LEAF):
        up = up + product(dot_nt, stacked(acc[l]), wh[l], wl[l])
    down = from_above(0)

    send_up(1, up + product(dot_nn, down, sh[...], sl[...]))
    finish(0, down)
    coefs(1)
    for side in range(2):
        coef_copy(1, side).start()
    send_halo(1)
    near_own()
    group(1)
    far_leaves(1)
    partials(1)
    near(1)
    finish(1, from_above(1))

    for pair in coupling_copies():
        for cp in pair:
            cp.wait_send()
    for p in range(2):
        for side in range(2):
            for i in range(LEAF):
                halo(p, side, i).wait_send()
            coef_copy(p, side).wait_send()
        for yy in y_peers:
            y_copy(p, yy, y).wait_send()
        for zz in z_peers:
            pz_copy(p, zz, z).wait_send()
            for yy in every_y:
                z_copy(p, zz, yy, z, y).wait_send()
        for xx in x_peers:
            px_copy(p, xx, x).wait_send()
            for yy in every_y:
                g_copy(p, xx, yy, x, y).wait_send()
        for zz in [z] + z_peers:
            forward(p, zz).wait_send()
        forward_top(p).wait_send()
        for l in range(LEAF):
            write(p, l).wait()


def hand_over(a, b, first, second, sem):
    copies = [pltpu.make_async_copy(a, first, sem.at[0]), pltpu.make_async_copy(b, second, sem.at[1])]
    for cp in copies:
        cp.start()
    for cp in copies:
        cp.wait()


def solution(mesh):
    leaf, grp = ("leaf", "grp")
    YN = mesh.shape[grp]
    XN = ZN = math.isqrt(mesh.shape[leaf] // 2)
    both = (leaf, grp)
    placed = (
        P(None, both),
        P(both, None),
        P(both, None, None, None),
        P(both, None, None),
        P(both, None),
        P(both, None, None, None),
        P(both, None, None),
        P(both, None, None),
        P(both, None),
        P(both, None, None, None),
        P(leaf, None),
        P(leaf, None, None, None),
    )

    def body(*refs):
        return kernel(ZN, XN, YN, *refs)

    hbm = pl.BlockSpec(memory_space=pl.ANY)
    anywhere = pl.BlockSpec(memory_space=pl.ANY)
    vmem = pltpu.VMEM
    dma = pltpu.SemaphoreType.DMA
    cols = LEAF * NODE
    scratch = [
        vmem((3, LEAF, RHS, NODE), F32),
        vmem((3 * LEAF, 2 * RHS, NODE), BF16),
        vmem((2, 2, LEAF, RHS, NODE), F32),
        vmem((LEAF, NEAR, NODE, NODE), F32),
        vmem((LEAF, NEAR, NODE, NODE), BF16),
        vmem((LEAF, NEAR, NODE, NODE), BF16),
        vmem((LEAF, RANK, NODE), F32),
        vmem((LEAF, RANK, NODE), BF16),
        vmem((LEAF, RANK, NODE), BF16),
        vmem((LEAF, LANES, NODE), BF16),
        vmem((LEAF, LANES, NODE), BF16),
        vmem((LANES, LANES), BF16),
        vmem((LANES, LANES), BF16),
        vmem((LEAF, RANK, RANK), F32),
        vmem((RANK, RANK), F32),
        vmem((LEAF, FAR, RANK, RANK), F32),
        vmem((LEAF, RANK, WIDE), BF16),
        vmem((LEAF, RANK, WIDE), BF16),
        vmem((FAR, RANK, RANK), F32),
        vmem((FAR, RANK, RANK), F32),
        vmem((XN, RANK, WIDE), F32),
        vmem((XN, RANK, WIDE), BF16),
        vmem((XN, RANK, WIDE), BF16),
        vmem((ZN, RANK, WIDE), F32),
        vmem((ZN, RANK, WIDE), BF16),
        vmem((ZN, RANK, WIDE), BF16),
        vmem((2, YN, 2, PACK, LANES), F32),
        vmem((2, XN, YN, PACK, LANES), F32),
        vmem((2, ZN, YN, PACK, LANES), F32),
        vmem((2, ZN, YN, PACK, LANES), F32),
        vmem((2, XN, PACK, LANES), F32),
        vmem((2, XN, PACK, LANES), F32),
        vmem((2, XN, PACK, LANES), F32),
        vmem((2, XN, PACK, LANES), F32),
        vmem((2, ZN, PACK, LANES), F32),
        vmem((2, ZN, PACK, LANES), F32),
        vmem((2, LEAF // 2, RHS, 2 * RANK), F32),
        vmem((2, 2, LEAF // 2, RHS, 2 * RANK), F32),
        vmem((3 * LEAF, RHS, 2 * RANK), F32),
        vmem((LEAF, RHS, NODE), F32),
        pltpu.SMEM((NEAR, LEAF), jnp.int32),
        pltpu.SMEM((LEAF, FAR), jnp.int32),
        pltpu.SMEM((XN, 1, FAR), jnp.int32),
        pltpu.SMEM((ZN, 1, FAR), jnp.int32),
        dma((10,)), dma((LEAF,)), dma((LEAF,)), dma((2, LEAF)),
        dma((2, 2, LEAF)), dma((2, 2, LEAF)),
        dma((2, 2)), dma((2, 2)),
        dma((2, YN)), dma((2, YN)),
        dma((2, ZN, YN)), dma((2, ZN, YN)),
        dma((2, XN, YN)), dma((2, XN, YN)),
        dma((2, ZN)), dma((2, ZN)), dma((2,)), dma((2,)),
        dma((2, XN)), dma((2, XN)),
        dma((2, ZN)), dma((2, ZN)),
        dma((XN,)), dma((XN,)), dma((ZN,)), dma((ZN,)),
        dma((XN,)), dma((XN,)), dma((ZN,)), dma((ZN,)),
    ]

    def per_device(signal, near_index, near_block, basis, *rest):
        args = (signal, near_index.T, near_block, jnp.swapaxes(basis, 1, 2), *rest)
        call = pl.pallas_call(
            body,
            out_shape=[jax.ShapeDtypeStruct((RHS, cols), F32)] * 2,
            in_specs=[hbm] * 12,
            out_specs=[anywhere, anywhere],
            scratch_shapes=scratch,
            compiler_params=pltpu.CompilerParams(
                collective_id=0, has_side_effects=True, vmem_limit_bytes=56 * 1024 * 1024
            ),
        )
        images = call(*args)
        final = pl.pallas_call(
            hand_over,
            out_shape=[jax.ShapeDtypeStruct((RHS, cols), F32)] * 2,
            in_specs=[pl.BlockSpec(memory_space=vmem)] * 2,
            out_specs=[hbm, hbm],
            scratch_shapes=[dma((2,))],
        )
        return tuple(final(*images))

    return jax.shard_map(
        per_device,
        mesh=mesh,
        in_specs=placed,
        out_specs=(P(None, both), P(None, both)),
        check_vma=False,
    )
```

```python
import math

import jax
import jax.numpy as jnp
from jax import lax
from jax.experimental import pallas as pl
from jax.experimental.pallas import tpu as pltpu
from jax.sharding import PartitionSpec as P

F32 = jnp.float32
BF16 = jnp.bfloat16
MESH = pl.DeviceIdType.MESH
LEAF = 8
NODE = 256
RANK = 64
RHS = 32
NEAR = 4
FAR = 8
WIDE = RANK * FAR
PACK = RHS // 2
LANES = 2 * RANK


def dot(a, b, da, db):
    return lax.dot_general(a, b, (((da,), (db,)), ((), ())), preferred_element_type=F32)


def dot_nt(a, b):
    return dot(a, b, 1, 1)


def dot_nn(a, b):
    return dot(a, b, 1, 0)


def dot_tn(a, b):
    return dot(a, b, 0, 0)


def split(t):
    hi = t.astype(BF16)
    return hi, (t - hi.astype(F32)).astype(BF16)


def stacked(t):
    return jnp.concatenate(split(t), axis=0)


def product(f, x, wh, wl):
    r = f(x, wh)
    return r[:RHS] + r[RHS:] + f(x[:RHS], wl)


def three(f, a, b):
    return f(a[0], b[0]) + f(a[1], b[0]) + f(a[0], b[1])


def swap(t):
    return pltpu.roll(t, RANK, 1)


def kernel(
    ZN, XN, YN,
    signal, near_hbm, near_block, basis, far0_hbm, coupling0, transfer1, transfer2,
    far1_index, coupling1, far2_index, coupling2,
    first, second,
    fld, xs, hf, na, ah, al, bs, bh, bl, wh, wl, sh, sl, t1, t2, c0, c0h, c0l,
    c1s, c2s, c1f, c1h, c1l, c2f, c2h, c2l,
    yb, lb, cba, cbb, gba, gbb, psx, pbx, psz, pbz, lcs, lch, lcd, acc, near_index, far0_index, si1, si2,
    in_sem, sig_sem, near_sem, out_sem, hs, hr, es, er, ys, yr, zs, zr, gs, gr, fs, fr, fgs, fgr,
    pxs, pxr, pzs, pzr, k1s, k1r, k2s, k2r, i1s, i1r, i2s, i2r,
):
    leaf = lax.axis_index("leaf")
    y = lax.axis_index("grp")
    c = lax.rem(leaf, 2)
    x = lax.rem(leaf // 2, XN)
    z = leaf // (2 * XN)
    leaves = 2 * XN * ZN
    cb, gb = (cba, cbb), (gba, gbb)
    low = lax.broadcasted_iota(jnp.int32, (RHS, LANES), 1) < RANK
    low_half = lax.broadcasted_iota(jnp.int32, (PACK, LANES), 1) < RANK
    half = LEAF // 2

    def at(zz, xx, cc, yy):
        return ((zz * XN + xx) * 2 + cc, yy)

    y_peers = [lax.rem(y + o, YN) for o in range(1, YN)]
    x_peers = [lax.rem(x + o, XN) for o in range(1, XN)]
    z_peers = [lax.rem(z + o, ZN) for o in range(1, ZN)]
    sibling = at(z, x, 1 - c, y)
    after = (lax.rem(leaf + (y + 1) // YN, leaves), lax.rem(y + 1, YN))
    before = (lax.rem(leaf + leaves - 1 + (y + YN - 1) // YN, leaves), lax.rem(y + YN - 1, YN))

    def remote(src, dst, ssem, rsem, dev):
        return pltpu.make_async_remote_copy(
            src_ref=src, dst_ref=dst, send_sem=ssem, recv_sem=rsem, device_id=dev, device_id_type=MESH
        )

    def pack(v):
        w = jnp.concatenate([v, jnp.zeros_like(v)], axis=1)
        return w[:PACK] + swap(w[PACK:])

    def pack_low(t):
        return jnp.where(low_half, t[:PACK], swap(t[PACK:]))

    def pack_high(t):
        return jnp.where(low_half, swap(t[:PACK]), t[PACK:])

    def pair_of(a, b):
        return jnp.where(
            low, jnp.concatenate([a, swap(a)], axis=0), jnp.concatenate([swap(b), b], axis=0)
        )

    def signal_load(i):
        return pltpu.make_async_copy(signal.at[:, pl.ds(i * NODE, NODE)], fld.at[0, i], sig_sem.at[i])

    def near_load(l):
        return pltpu.make_async_copy(near_block.at[l], na.at[l], near_sem.at[l])

    loads = []
    for n, (src, dst) in enumerate((
        (basis, bs), (transfer1, t1), (transfer2.at[0], t2),
        (far1_index, si1.at[x]), (far2_index, si2.at[z]), (coupling1.at[0], c1s), (coupling2.at[0], c2s),
        (coupling0, c0), (near_hbm, near_index), (far0_hbm, far0_index),
    )):
        loads.append(pltpu.make_async_copy(src, dst, in_sem.at[n]))
    for cp in loads[:3]:
        cp.start()
    for i in range(LEAF):
        signal_load(i).start()

    every_y = [lax.rem(y + o, YN) for o in range(YN)]
    greet = [at(zz, x, c, yy) for zz in z_peers[1:2] + z_peers[:1] + z_peers[2:] for yy in every_y]
    greet += [at(z, xx, c, yy) for xx in x_peers[1:2] + x_peers[:1] + x_peers[2:] for yy in every_y]
    greet += [at(z, x, c, yy) for yy in y_peers] + [sibling, after, before]
    barrier = pltpu.get_barrier_semaphore()
    for dev in greet:
        pl.semaphore_signal(barrier, inc=1, device_id=dev, device_id_type=MESH)

    for cp in loads[3:]:
        cp.start()
    for l in range(LEAF):
        near_load(l).start()

    def halo(p, side, i):
        return remote(
            fld.at[p, i], hf.at[p, side, i], hs.at[p, side, i], hr.at[p, side, i], after if side == 0 else before
        )

    def send_halo(p):
        for i in range(LEAF):
            halo(p, 0, LEAF - 1 - i).start()
            halo(p, 1, i).start()

    def coupling_copies():
        out = [
            (remote(c1f.at[x], c1f.at[x], k1s.at[xx], k1r.at[x], at(z, xx, c, y)),
             remote(si1.at[x], si1.at[x], i1s.at[xx], i1r.at[x], at(z, xx, c, y)))
            for xx in x_peers
        ]
        out += [
            (remote(c2f.at[z], c2f.at[z], k2s.at[zz], k2r.at[z], at(zz, x, c, y)),
             remote(si2.at[z], si2.at[z], i2s.at[zz], i2r.at[z], at(zz, x, c, y)))
            for zz in z_peers
        ]
        return out

    base = (leaf * YN + y) * LEAF - LEAF

    def near_split(l, carry):
        near_load(l).wait()
        for k in range(NEAR):
            ah[l, k], al[l, k] = split(na[l, k])
        return carry

    def near_own():
        for l in range(LEAF):
            acc[l] = product(dot_nt, xs[LEAF + l], ah[l, 0], al[l, 0])

    def coupling_split(l, carry):
        for j in range(FAR // 2):
            hi, lo = split(jnp.concatenate([c0[l, 2 * j], c0[l, 2 * j + 1]], axis=1))
            c0h[l, :, pl.ds(j * LANES, LANES)] = hi
            c0l[l, :, pl.ds(j * LANES, LANES)] = lo
        return carry

    def coef_copy(p, side):
        return remote(lcs.at[p], lch.at[p, side], es.at[p, side], er.at[p, side], after if side == 0 else before)

    def y_copy(p, yy, slot):
        return remote(yb.at[p, slot], yb.at[p, slot], ys.at[p, yy], yr.at[p, slot], at(z, x, c, yy))

    def z_copy(p, zz, yy, slot_z, slot_y):
        return remote(
            yb.at[p, y, 0], cb[p].at[0, slot_z, slot_y], zs.at[p, zz, yy], zr.at[p, slot_z, slot_y], at(zz, x, c, yy)
        )

    def g_copy(p, xx, yy, slot_x, slot_y):
        return remote(
            yb.at[p, y, 1], lb.at[p, slot_x, slot_y], gs.at[p, xx, yy], gr.at[p, slot_x, slot_y], at(z, xx, c, yy)
        )

    def forward(p, zz):
        return remote(cb[p].at[0, zz], cb[p].at[1, zz], fs.at[p, zz], fr.at[p, zz], sibling)

    def forward_top(p):
        return remote(gb[p].at[0], gb[p].at[1], fgs.at[p], fgr.at[p], sibling)

    def px_copy(p, xx, slot):
        return remote(psx.at[p, xx], pbx.at[p, slot], pxs.at[p, xx], pxr.at[p, slot], at(z, xx, c, y))

    def pz_copy(p, zz, slot):
        return remote(psz.at[p, zz], pbz.at[p, slot], pzs.at[p, zz], pzr.at[p, slot], at(zz, x, c, y))

    def wide(i):
        return jnp.minimum(jnp.maximum(i - base, 0), 3 * LEAF - 1)

    def slot_of(cc):
        return jnp.where(cc == c, 0, 1)

    def mid_tile(p, m, k):
        i = si1[m, 0, k]
        g = lax.div(i, YN)
        h = lax.div(g, 2)
        t = cb[p][slot_of(lax.rem(g, 2)), lax.div(h, XN), lax.rem(i, YN)]
        return jnp.where(lax.rem(h, XN) == x, t, 0.0)

    def top_tile(p, m, k):
        i = si2[m, 0, k]
        h = lax.div(i, 2)
        t = gb[p][slot_of(lax.rem(i, 2)), lax.rem(h, XN)]
        return jnp.where(lax.div(h, XN) == z, t, 0.0)

    def leaf_tile(l, k):
        return lcd[wide(far0_index[l, k])]

    def picked(pair):
        return jnp.concatenate([stacked(pair(j)) for j in range(FAR // 2)], axis=1)

    def coefs(p):
        for j in range(half):
            pair = jnp.concatenate(
                [product(dot_nt, xs[LEAF + l], bh[l], bl[l]) for l in (2 * j, 2 * j + 1)], axis=1
            )
            other = swap(pair)
            lcs[p, j] = pair
            lcd[LEAF + 2 * j] = jnp.where(low, pair, other)
            lcd[LEAF + 2 * j + 1] = jnp.where(low, other, pair)

    def send_up(p, u):
        yb[p, y, 0] = pack_low(u)
        yb[p, y, 1] = pack_high(u)
        for xx, zz in zip(x_peers, z_peers):
            for yy in every_y[1:] + every_y[:1]:
                g_copy(p, xx, yy, x, y).start()
                z_copy(p, zz, yy, z, y).start()
        for yy in y_peers:
            y_copy(p, yy, y).start()

    def group(p):
        for yy in y_peers:
            y_copy(p, yy, yy).wait_recv()
        total = yb[p, 0, 1]
        for i in range(1, YN):
            total = total + yb[p, i, 1]
        gb[p][0, x] = total
        for i in range(YN):
            cb[p][0, z, i] = yb[p, i, 0]
        forward(p, z).start()
        for xx in x_peers:
            for yy in every_y:
                g_copy(p, xx, yy, xx, yy).wait_recv()
            total = lb[p, xx, 0]
            for i in range(1, YN):
                total = total + lb[p, xx, i]
            gb[p][0, xx] = total
        forward_top(p).start()
        for zz in z_peers:
            for yy in every_y:
                z_copy(p, zz, yy, zz, yy).wait_recv()
            forward(p, zz).start()

    def far_leaves(p):
        for side in range(2):
            coef_copy(p, side).wait_recv()
        for j in range(half):
            for side in range(2):
                t = lch[p, side, j]
                r = swap(t)
                lcd[side * 2 * LEAF + 2 * j] = jnp.where(low, t, r)
                lcd[side * 2 * LEAF + 2 * j + 1] = jnp.where(low, r, t)

        tiles = [
            picked(lambda j: jnp.where(low, leaf_tile(l, 2 * j), leaf_tile(l, 2 * j + 1))) for l in range(LEAF)
        ]
        sums = [stacked(product(dot_nt, tiles[l], c0h[l], c0l[l])) for l in range(LEAF)]
        for l in range(LEAF):
            acc[l] += product(dot_nn, sums[l], bh[l], bl[l])

    def partials(p):
        for zz in [z] + z_peers:
            forward(p, zz).wait_recv()
        forward_top(p).wait_recv()
        for m in range(XN):
            v = picked(lambda j: pair_of(mid_tile(p, m, 2 * j), mid_tile(p, m, 2 * j + 1)))
            psx[p, m] = pack(product(dot_nt, v, c1h[m], c1l[m]))
        for xx in x_peers:
            px_copy(p, xx, x).start()
        for m in range(ZN):
            v = picked(lambda j: pair_of(top_tile(p, m, 2 * j), top_tile(p, m, 2 * j + 1)))
            psz[p, m] = pack(product(dot_nt, v, c2h[m], c2l[m]))
        for zz in z_peers:
            pz_copy(p, zz, z).start()

    def near(p):
        def take(side, i):
            halo(p, side, i).wait_recv()
            xs[side * 2 * LEAF + i] = stacked(hf[p, side, i])

        def near_leaf(l):
            total = acc[l]
            for k in range(1, NEAR):
                total = total + product(dot_nt, xs[wide(near_index[k, l])], ah[l, k], al[l, k])
            acc[l] = total

        def take_first(i, carry):
            take(0, LEAF - 1 - i)
            take(1, i)
            return carry

        lax.fori_loop(0, half, take_first, 0)

        def near_pair(j, carry):
            take(0, half - 1 - j)
            take(1, half + j)
            near_leaf(half - 1 - j)
            near_leaf(half + j)
            return carry

        lax.fori_loop(0, half, near_pair, 0)

    def from_above(p):
        for xx in x_peers:
            px_copy(p, xx, xx).wait_recv()
        for zz in z_peers:
            pz_copy(p, zz, zz).wait_recv()
        mid = psx[p, x]
        for xx in x_peers:
            mid = mid + pbx[p, xx]
        top = psz[p, z]
        for zz in z_peers:
            top = top + pbz[p, zz]
        return stacked(pair_of(mid, top))

    def write(p, l):
        out = first if p == 0 else second
        return pltpu.make_async_copy(fld.at[p + 1, l], out.at[:, pl.ds(l * NODE, NODE)], out_sem.at[p, l])

    def finish(p, down):
        for l in range(LEAF):
            v = acc[l] + product(dot_nn, down, wh[l], wl[l])
            fld[p + 1, l] = v
            if p == 0:
                xs[LEAF + l] = stacked(v)
        for l in range(LEAF):
            write(p, l).start()

    for i in range(LEAF):
        signal_load(i).wait()
    for cp in loads[:3]:
        cp.wait()
    for l in range(LEAF):
        bh[l], bl[l] = split(bs[l])
        xs[LEAF + l] = stacked(fld[0, l])
    coefs(0)
    t1p = split(t1[...].reshape(WIDE, RANK))
    t2p = split(t2[...])
    low_level = jnp.concatenate([stacked(lcs[0, j]) for j in range(half)], axis=1)
    cluster = product(dot_nn, low_level, *t1p)
    up = jnp.concatenate([cluster, product(dot_nn, stacked(cluster), *t2p)], axis=1)

    pl.semaphore_wait(barrier, len(greet))
    send_up(0, up)
    for side in range(2):
        coef_copy(0, side).start()
    for cp in loads[3:7]:
        cp.wait()
    for j in range(FAR // 2):
        c1f[x, :, pl.ds(j * LANES, LANES)] = jnp.concatenate([c1s[2 * j], c1s[2 * j + 1]], axis=1)
        c2f[z, :, pl.ds(j * LANES, LANES)] = jnp.concatenate([c2s[2 * j], c2s[2 * j + 1]], axis=1)
    for pair in coupling_copies():
        for cp in pair:
            cp.start()
    send_halo(0)

    for l in range(LEAF):
        xs[l] = jnp.zeros((2 * RHS, NODE), BF16)
        xs[2 * LEAF + l] = jnp.zeros((2 * RHS, NODE), BF16)
    lax.fori_loop(0, LEAF, near_split, 0)
    group(0)

    t1a, t1b = split(t1[...].reshape(WIDE, RANK))
    t12 = three(dot_nn, (t1a, t1b), split(t2[...]))
    for l in range(LEAF):
        e = split(jnp.concatenate([t1[l], t12[l * RANK:(l + 1) * RANK]], axis=1))
        wh[l], wl[l] = split(three(dot_tn, e, (bh[l], bl[l])))
    for cp in loads[7:]:
        cp.wait()
    lax.fori_loop(0, LEAF, coupling_split, 0)
    near_own()
    square = three(dot_nt, (wh[0], wl[0]), (wh[0], wl[0]))
    for l in range(1, LEAF):
        square = square + three(dot_nt, (wh[l], wl[l]), (wh[l], wl[l]))
    sh[...], sl[...] = split(square)
    far_leaves(0)
    for xx in x_peers:
        remote(c1f.at[xx], c1f.at[xx], k1s.at[xx], k1r.at[xx], at(z, xx, c, y)).wait_recv()
        remote(si1.at[xx], si1.at[xx], i1s.at[xx], i1r.at[xx], at(z, xx, c, y)).wait_recv()
    for zz in z_peers:
        remote(c2f.at[zz], c2f.at[zz], k2s.at[zz], k2r.at[zz], at(zz, x, c, y)).wait_recv()
        remote(si2.at[zz], si2.at[zz], i2s.at[zz], i2r.at[zz], at(zz, x, c, y)).wait_recv()
    for m in range(XN):
        c1h[m], c1l[m] = split(c1f[m])
    for m in range(ZN):
        c2h[m], c2l[m] = split(c2f[m])
    partials(0)
    near(0)
    up = product(dot_nt, stacked(acc[0]), wh[0], wl[0])
    for l in range(1, LEAF):
        up = up + product(dot_nt, stacked(acc[l]), wh[l], wl[l])
    down = from_above(0)

    send_up(1, up + product(dot_nn, down, sh[...], sl[...]))
    finish(0, down)
    coefs(1)
    for side in range(2):
        coef_copy(1, side).start()
    send_halo(1)
    near_own()
    group(1)
    far_leaves(1)
    partials(1)
    near(1)
    finish(1, from_above(1))

    for pair in coupling_copies():
        for cp in pair:
            cp.wait_send()
    for p in range(2):
        for side in range(2):
            for i in range(LEAF):
                halo(p, side, i).wait_send()
            coef_copy(p, side).wait_send()
        for yy in y_peers:
            y_copy(p, yy, y).wait_send()
        for zz in z_peers:
            pz_copy(p, zz, z).wait_send()
            for yy in every_y:
                z_copy(p, zz, yy, z, y).wait_send()
        for xx in x_peers:
            px_copy(p, xx, x).wait_send()
            for yy in every_y:
                g_copy(p, xx, yy, x, y).wait_send()
        for zz in [z] + z_peers:
            forward(p, zz).wait_send()
        forward_top(p).wait_send()
        for l in range(LEAF):
            write(p, l).wait()


def hand_over(a, b, first, second, sem):
    copies = [pltpu.make_async_copy(a, first, sem.at[0]), pltpu.make_async_copy(b, second, sem.at[1])]
    for cp in copies:
        cp.start()
    for cp in copies:
        cp.wait()


def solution(mesh):
    leaf, grp = ("leaf", "grp")
    YN = mesh.shape[grp]
    XN = ZN = math.isqrt(mesh.shape[leaf] // 2)
    both = (leaf, grp)
    placed = (
        P(None, both),
        P(both, None),
        P(both, None, None, None),
        P(both, None, None),
        P(both, None),
        P(both, None, None, None),
        P(both, None, None),
        P(both, None, None),
        P(both, None),
        P(both, None, None, None),
        P(leaf, None),
        P(leaf, None, None, None),
    )

    def body(*refs):
        return kernel(ZN, XN, YN, *refs)

    hbm = pl.BlockSpec(memory_space=pl.ANY)
    anywhere = pl.BlockSpec(memory_space=pl.ANY)
    vmem = pltpu.VMEM
    dma = pltpu.SemaphoreType.DMA
    cols = LEAF * NODE
    scratch = [
        vmem((3, LEAF, RHS, NODE), F32),
        vmem((3 * LEAF, 2 * RHS, NODE), BF16),
        vmem((2, 2, LEAF, RHS, NODE), F32),
        vmem((LEAF, NEAR, NODE, NODE), F32),
        vmem((LEAF, NEAR, NODE, NODE), BF16),
        vmem((LEAF, NEAR, NODE, NODE), BF16),
        vmem((LEAF, RANK, NODE), F32),
        vmem((LEAF, RANK, NODE), BF16),
        vmem((LEAF, RANK, NODE), BF16),
        vmem((LEAF, LANES, NODE), BF16),
        vmem((LEAF, LANES, NODE), BF16),
        vmem((LANES, LANES), BF16),
        vmem((LANES, LANES), BF16),
        vmem((LEAF, RANK, RANK), F32),
        vmem((RANK, RANK), F32),
        vmem((LEAF, FAR, RANK, RANK), F32),
        vmem((LEAF, RANK, WIDE), BF16),
        vmem((LEAF, RANK, WIDE), BF16),
        vmem((FAR, RANK, RANK), F32),
        vmem((FAR, RANK, RANK), F32),
        vmem((XN, RANK, WIDE), F32),
        vmem((XN, RANK, WIDE), BF16),
        vmem((XN, RANK, WIDE), BF16),
        vmem((ZN, RANK, WIDE), F32),
        vmem((ZN, RANK, WIDE), BF16),
        vmem((ZN, RANK, WIDE), BF16),
        vmem((2, YN, 2, PACK, LANES), F32),
        vmem((2, XN, YN, PACK, LANES), F32),
        vmem((2, ZN, YN, PACK, LANES), F32),
        vmem((2, ZN, YN, PACK, LANES), F32),
        vmem((2, XN, PACK, LANES), F32),
        vmem((2, XN, PACK, LANES), F32),
        vmem((2, XN, PACK, LANES), F32),
        vmem((2, XN, PACK, LANES), F32),
        vmem((2, ZN, PACK, LANES), F32),
        vmem((2, ZN, PACK, LANES), F32),
        vmem((2, LEAF // 2, RHS, 2 * RANK), F32),
        vmem((2, 2, LEAF // 2, RHS, 2 * RANK), F32),
        vmem((3 * LEAF, RHS, 2 * RANK), F32),
        vmem((LEAF, RHS, NODE), F32),
        pltpu.SMEM((NEAR, LEAF), jnp.int32),
        pltpu.SMEM((LEAF, FAR), jnp.int32),
        pltpu.SMEM((XN, 1, FAR), jnp.int32),
        pltpu.SMEM((ZN, 1, FAR), jnp.int32),
        dma((10,)), dma((LEAF,)), dma((LEAF,)), dma((2, LEAF)),
        dma((2, 2, LEAF)), dma((2, 2, LEAF)),
        dma((2, 2)), dma((2, 2)),
        dma((2, YN)), dma((2, YN)),
        dma((2, ZN, YN)), dma((2, ZN, YN)),
        dma((2, XN, YN)), dma((2, XN, YN)),
        dma((2, ZN)), dma((2, ZN)), dma((2,)), dma((2,)),
        dma((2, XN)), dma((2, XN)),
        dma((2, ZN)), dma((2, ZN)),
        dma((XN,)), dma((XN,)), dma((ZN,)), dma((ZN,)),
        dma((XN,)), dma((XN,)), dma((ZN,)), dma((ZN,)),
    ]

    def per_device(signal, near_index, near_block, basis, *rest):
        args = (signal, near_index.T, near_block, jnp.swapaxes(basis, 1, 2), *rest)
        call = pl.pallas_call(
            body,
            out_shape=[jax.ShapeDtypeStruct((RHS, cols), F32)] * 2,
            in_specs=[hbm] * 12,
            out_specs=[anywhere, anywhere],
            scratch_shapes=scratch,
            compiler_params=pltpu.CompilerParams(
                collective_id=0, has_side_effects=True, vmem_limit_bytes=56 * 1024 * 1024
            ),
        )
        images = call(*args)
        final = pl.pallas_call(
            hand_over,
            out_shape=[jax.ShapeDtypeStruct((RHS, cols), F32)] * 2,
            in_specs=[pl.BlockSpec(memory_space=vmem)] * 2,
            out_specs=[hbm, hbm],
            scratch_shapes=[dma((2,))],
        )
        return tuple(final(*images))

    return jax.shard_map(
        per_device,
        mesh=mesh,
        in_specs=placed,
        out_specs=(P(None, both), P(None, both)),
        check_vma=False,
    )
```

```python
import math

import jax
import jax.numpy as jnp
from jax import lax
from jax.experimental import pallas as pl
from jax.experimental.pallas import tpu as pltpu
from jax.sharding import PartitionSpec as P

F32 = jnp.float32
BF16 = jnp.bfloat16
MESH = pl.DeviceIdType.MESH
LEAF = 8
NODE = 256
RANK = 64
RHS = 32
NEAR = 4
FAR = 8
WIDE = RANK * FAR
PACK = RHS // 2
LANES = 2 * RANK


def dot(a, b, da, db):
    return lax.dot_general(a, b, (((da,), (db,)), ((), ())), preferred_element_type=F32)


def dot_nt(a, b):
    return dot(a, b, 1, 1)


def dot_nn(a, b):
    return dot(a, b, 1, 0)


def dot_tn(a, b):
    return dot(a, b, 0, 0)


def split(t):
    hi = t.astype(BF16)
    return hi, (t - hi.astype(F32)).astype(BF16)


def stacked(t):
    return jnp.concatenate(split(t), axis=0)


def product(f, x, wh, wl):
    r = f(x, wh)
    return r[:RHS] + r[RHS:] + f(x[:RHS], wl)


def three(f, a, b):
    return f(a[0], b[0]) + f(a[1], b[0]) + f(a[0], b[1])


def swap(t):
    return pltpu.roll(t, RANK, 1)


def kernel(
    ZN, XN, YN,
    signal, near_hbm, near_block, basis, far0_hbm, coupling0, transfer1, transfer2,
    far1_index, coupling1, far2_index, coupling2,
    first, second,
    fld, xs, hf, na, ah, al, bs, bh, bl, wh, wl, sh, sl, t1, t2, c0, c0h, c0l,
    c1s, c2s, c1f, c1h, c1l, c2f, c2h, c2l,
    yb, lb, cba, cbb, gba, gbb, psx, pbx, psz, pbz, lcs, lch, lcd, acc, near_index, far0_index, si1, si2,
    in_sem, sig_sem, near_sem, out_sem, hs, hr, es, er, ys, yr, zs, zr, gs, gr, fs, fr, fgs, fgr,
    pxs, pxr, pzs, pzr, k1s, k1r, k2s, k2r, i1s, i1r, i2s, i2r,
):
    leaf = lax.axis_index("leaf")
    y = lax.axis_index("grp")
    c = lax.rem(leaf, 2)
    x = lax.rem(leaf // 2, XN)
    z = leaf // (2 * XN)
    leaves = 2 * XN * ZN
    cb, gb = (cba, cbb), (gba, gbb)
    low = lax.broadcasted_iota(jnp.int32, (RHS, LANES), 1) < RANK
    low_half = lax.broadcasted_iota(jnp.int32, (PACK, LANES), 1) < RANK
    half = LEAF // 2

    def at(zz, xx, cc, yy):
        return ((zz * XN + xx) * 2 + cc, yy)

    y_peers = [lax.rem(y + o, YN) for o in range(1, YN)]
    x_peers = [lax.rem(x + o, XN) for o in range(1, XN)]
    z_peers = [lax.rem(z + o, ZN) for o in range(1, ZN)]
    sibling = at(z, x, 1 - c, y)
    after = (lax.rem(leaf + (y + 1) // YN, leaves), lax.rem(y + 1, YN))
    before = (lax.rem(leaf + leaves - 1 + (y + YN - 1) // YN, leaves), lax.rem(y + YN - 1, YN))

    def remote(src, dst, ssem, rsem, dev):
        return pltpu.make_async_remote_copy(
            src_ref=src, dst_ref=dst, send_sem=ssem, recv_sem=rsem, device_id=dev, device_id_type=MESH
        )

    def pack(v):
        w = jnp.concatenate([v, jnp.zeros_like(v)], axis=1)
        return w[:PACK] + swap(w[PACK:])

    def pack_low(t):
        return jnp.where(low_half, t[:PACK], swap(t[PACK:]))

    def pack_high(t):
        return jnp.where(low_half, swap(t[:PACK]), t[PACK:])

    def pair_of(a, b):
        return jnp.where(
            low, jnp.concatenate([a, swap(a)], axis=0), jnp.concatenate([swap(b), b], axis=0)
        )

    def signal_load(i):
        return pltpu.make_async_copy(signal.at[:, pl.ds(i * NODE, NODE)], fld.at[0, i], sig_sem.at[i])

    def near_load(l):
        return pltpu.make_async_copy(near_block.at[l], na.at[l], near_sem.at[l])

    loads = []
    for n, (src, dst) in enumerate((
        (basis, bs), (transfer1, t1), (transfer2.at[0], t2),
        (far1_index, si1.at[x]), (far2_index, si2.at[z]), (coupling1.at[0], c1s), (coupling2.at[0], c2s),
        (coupling0, c0), (near_hbm, near_index), (far0_hbm, far0_index),
    )):
        loads.append(pltpu.make_async_copy(src, dst, in_sem.at[n]))
    for cp in loads[:3]:
        cp.start()
    for i in range(LEAF):
        signal_load(i).start()

    every_y = [lax.rem(y + o, YN) for o in range(YN)]
    greet = [at(zz, x, c, yy) for zz in z_peers[1:2] + z_peers[:1] + z_peers[2:] for yy in every_y]
    greet += [at(z, xx, c, yy) for xx in x_peers[1:2] + x_peers[:1] + x_peers[2:] for yy in every_y]
    greet += [at(z, x, c, yy) for yy in y_peers] + [sibling, after, before]
    barrier = pltpu.get_barrier_semaphore()
    for dev in greet:
        pl.semaphore_signal(barrier, inc=1, device_id=dev, device_id_type=MESH)

    for cp in loads[3:7]:
        cp.start()

    def halo(p, side, i):
        return remote(
            fld.at[p, i], hf.at[p, side, i], hs.at[p, side, i], hr.at[p, side, i], after if side == 0 else before
        )

    def send_halo(p):
        for i in range(LEAF):
            halo(p, 0, LEAF - 1 - i).start()
            halo(p, 1, i).start()

    def coupling_copies():
        out = [
            (remote(c1f.at[x], c1f.at[x], k1s.at[xx], k1r.at[x], at(z, xx, c, y)),
             remote(si1.at[x], si1.at[x], i1s.at[xx], i1r.at[x], at(z, xx, c, y)))
            for xx in x_peers
        ]
        out += [
            (remote(c2f.at[z], c2f.at[z], k2s.at[zz], k2r.at[z], at(zz, x, c, y)),
             remote(si2.at[z], si2.at[z], i2s.at[zz], i2r.at[z], at(zz, x, c, y)))
            for zz in z_peers
        ]
        return out

    base = (leaf * YN + y) * LEAF - LEAF

    def near_split(l, carry):
        near_load(l).wait()
        for k in range(NEAR):
            ah[l, k], al[l, k] = split(na[l, k])
        return carry

    def near_own():
        for l in range(LEAF):
            acc[l] = product(dot_nt, xs[LEAF + l], ah[l, 0], al[l, 0])

    def coupling_split(l, carry):
        for j in range(FAR // 2):
            hi, lo = split(jnp.concatenate([c0[l, 2 * j], c0[l, 2 * j + 1]], axis=1))
            c0h[l, :, pl.ds(j * LANES, LANES)] = hi
            c0l[l, :, pl.ds(j * LANES, LANES)] = lo
        return carry

    def coef_copy(p, side):
        return remote(lcs.at[p], lch.at[p, side], es.at[p, side], er.at[p, side], after if side == 0 else before)

    def y_copy(p, yy, slot):
        return remote(yb.at[p, slot], yb.at[p, slot], ys.at[p, yy], yr.at[p, slot], at(z, x, c, yy))

    def z_copy(p, zz, yy, slot_z, slot_y):
        return remote(
            yb.at[p, y, 0], cb[p].at[0, slot_z, slot_y], zs.at[p, zz, yy], zr.at[p, slot_z, slot_y], at(zz, x, c, yy)
        )

    def g_copy(p, xx, yy, slot_x, slot_y):
        return remote(
            yb.at[p, y, 1], lb.at[p, slot_x, slot_y], gs.at[p, xx, yy], gr.at[p, slot_x, slot_y], at(z, xx, c, yy)
        )

    def forward(p, zz):
        return remote(cb[p].at[0, zz], cb[p].at[1, zz], fs.at[p, zz], fr.at[p, zz], sibling)

    def forward_top(p):
        return remote(gb[p].at[0], gb[p].at[1], fgs.at[p], fgr.at[p], sibling)

    def px_copy(p, xx, slot):
        return remote(psx.at[p, xx], pbx.at[p, slot], pxs.at[p, xx], pxr.at[p, slot], at(z, xx, c, y))

    def pz_copy(p, zz, slot):
        return remote(psz.at[p, zz], pbz.at[p, slot], pzs.at[p, zz], pzr.at[p, slot], at(zz, x, c, y))

    def wide(i):
        return jnp.minimum(jnp.maximum(i - base, 0), 3 * LEAF - 1)

    def slot_of(cc):
        return jnp.where(cc == c, 0, 1)

    def mid_tile(p, m, k):
        i = si1[m, 0, k]
        g = lax.div(i, YN)
        h = lax.div(g, 2)
        t = cb[p][slot_of(lax.rem(g, 2)), lax.div(h, XN), lax.rem(i, YN)]
        return jnp.where(lax.rem(h, XN) == x, t, 0.0)

    def top_tile(p, m, k):
        i = si2[m, 0, k]
        h = lax.div(i, 2)
        t = gb[p][slot_of(lax.rem(i, 2)), lax.rem(h, XN)]
        return jnp.where(lax.div(h, XN) == z, t, 0.0)

    def leaf_tile(l, k):
        return lcd[wide(far0_index[l, k])]

    def picked(pair):
        return jnp.concatenate([stacked(pair(j)) for j in range(FAR // 2)], axis=1)

    def coefs(p):
        for j in range(half):
            pair = jnp.concatenate(
                [product(dot_nt, xs[LEAF + l], bh[l], bl[l]) for l in (2 * j, 2 * j + 1)], axis=1
            )
            other = swap(pair)
            lcs[p, j] = pair
            lcd[LEAF + 2 * j] = jnp.where(low, pair, other)
            lcd[LEAF + 2 * j + 1] = jnp.where(low, other, pair)

    def send_up(p, u):
        yb[p, y, 0] = pack_low(u)
        yb[p, y, 1] = pack_high(u)
        for xx, zz in zip(x_peers, z_peers):
            for yy in every_y[1:] + every_y[:1]:
                g_copy(p, xx, yy, x, y).start()
                z_copy(p, zz, yy, z, y).start()
        for yy in y_peers:
            y_copy(p, yy, y).start()

    def group(p):
        for yy in y_peers:
            y_copy(p, yy, yy).wait_recv()
        total = yb[p, 0, 1]
        for i in range(1, YN):
            total = total + yb[p, i, 1]
        gb[p][0, x] = total
        for i in range(YN):
            cb[p][0, z, i] = yb[p, i, 0]
        forward(p, z).start()
        for xx in x_peers:
            for yy in every_y:
                g_copy(p, xx, yy, xx, yy).wait_recv()
            total = lb[p, xx, 0]
            for i in range(1, YN):
                total = total + lb[p, xx, i]
            gb[p][0, xx] = total
        forward_top(p).start()
        for zz in z_peers:
            for yy in every_y:
                z_copy(p, zz, yy, zz, yy).wait_recv()
            forward(p, zz).start()

    def far_leaves(p):
        for side in range(2):
            coef_copy(p, side).wait_recv()
        for j in range(half):
            for side in range(2):
                t = lch[p, side, j]
                r = swap(t)
                lcd[side * 2 * LEAF + 2 * j] = jnp.where(low, t, r)
                lcd[side * 2 * LEAF + 2 * j + 1] = jnp.where(low, r, t)

        tiles = [
            picked(lambda j: jnp.where(low, leaf_tile(l, 2 * j), leaf_tile(l, 2 * j + 1))) for l in range(LEAF)
        ]
        sums = [stacked(product(dot_nt, tiles[l], c0h[l], c0l[l])) for l in range(LEAF)]
        for l in range(LEAF):
            acc[l] += product(dot_nn, sums[l], bh[l], bl[l])

    def partials(p):
        for zz in [z] + z_peers:
            forward(p, zz).wait_recv()
        forward_top(p).wait_recv()
        for m in range(XN):
            v = picked(lambda j: pair_of(mid_tile(p, m, 2 * j), mid_tile(p, m, 2 * j + 1)))
            psx[p, m] = pack(product(dot_nt, v, c1h[m], c1l[m]))
        for xx in x_peers:
            px_copy(p, xx, x).start()
        for m in range(ZN):
            v = picked(lambda j: pair_of(top_tile(p, m, 2 * j), top_tile(p, m, 2 * j + 1)))
            psz[p, m] = pack(product(dot_nt, v, c2h[m], c2l[m]))
        for zz in z_peers:
            pz_copy(p, zz, z).start()

    def near(p):
        def take(side, i):
            halo(p, side, i).wait_recv()
            xs[side * 2 * LEAF + i] = stacked(hf[p, side, i])

        def near_leaf(l):
            total = acc[l]
            for k in range(1, NEAR):
                total = total + product(dot_nt, xs[wide(near_index[k, l])], ah[l, k], al[l, k])
            acc[l] = total

        def take_first(i, carry):
            take(0, LEAF - 1 - i)
            take(1, i)
            return carry

        lax.fori_loop(0, half, take_first, 0)

        def near_pair(j, carry):
            take(0, half - 1 - j)
            take(1, half + j)
            near_leaf(half - 1 - j)
            near_leaf(half + j)
            return carry

        lax.fori_loop(0, half, near_pair, 0)

    def from_above(p):
        for xx in x_peers:
            px_copy(p, xx, xx).wait_recv()
        for zz in z_peers:
            pz_copy(p, zz, zz).wait_recv()
        mid = psx[p, x]
        for xx in x_peers:
            mid = mid + pbx[p, xx]
        top = psz[p, z]
        for zz in z_peers:
            top = top + pbz[p, zz]
        return stacked(pair_of(mid, top))

    def write(p, l):
        out = first if p == 0 else second
        return pltpu.make_async_copy(fld.at[p + 1, l], out.at[:, pl.ds(l * NODE, NODE)], out_sem.at[p, l])

    def finish(p, down):
        for l in range(LEAF):
            v = acc[l] + product(dot_nn, down, wh[l], wl[l])
            fld[p + 1, l] = v
            if p == 0:
                xs[LEAF + l] = stacked(v)
        for l in range(LEAF):
            write(p, l).start()

    for i in range(LEAF):
        signal_load(i).wait()
    for cp in loads[:3]:
        cp.wait()
    for l in range(LEAF):
        bh[l], bl[l] = split(bs[l])
        xs[LEAF + l] = stacked(fld[0, l])
    coefs(0)
    t1p = split(t1[...].reshape(WIDE, RANK))
    t2p = split(t2[...])
    low_level = jnp.concatenate([stacked(lcs[0, j]) for j in range(half)], axis=1)
    cluster = product(dot_nn, low_level, *t1p)
    up = jnp.concatenate([cluster, product(dot_nn, stacked(cluster), *t2p)], axis=1)

    pl.semaphore_wait(barrier, len(greet))
    send_up(0, up)
    for l in range(LEAF):
        near_load(l).start()
    for cp in loads[7:]:
        cp.start()
    for side in range(2):
        coef_copy(0, side).start()
    for cp in loads[3:7]:
        cp.wait()
    for j in range(FAR // 2):
        c1f[x, :, pl.ds(j * LANES, LANES)] = jnp.concatenate([c1s[2 * j], c1s[2 * j + 1]], axis=1)
        c2f[z, :, pl.ds(j * LANES, LANES)] = jnp.concatenate([c2s[2 * j], c2s[2 * j + 1]], axis=1)
    for pair in coupling_copies():
        for cp in pair:
            cp.start()
    send_halo(0)

    for l in range(LEAF):
        xs[l] = jnp.zeros((2 * RHS, NODE), BF16)
        xs[2 * LEAF + l] = jnp.zeros((2 * RHS, NODE), BF16)
    lax.fori_loop(0, LEAF, near_split, 0)
    group(0)

    t1a, t1b = split(t1[...].reshape(WIDE, RANK))
    t12 = three(dot_nn, (t1a, t1b), split(t2[...]))
    for l in range(LEAF):
        e = split(jnp.concatenate([t1[l], t12[l * RANK:(l + 1) * RANK]], axis=1))
        wh[l], wl[l] = split(three(dot_tn, e, (bh[l], bl[l])))
    for cp in loads[7:]:
        cp.wait()
    lax.fori_loop(0, LEAF, coupling_split, 0)
    near_own()
    square = three(dot_nt, (wh[0], wl[0]), (wh[0], wl[0]))
    for l in range(1, LEAF):
        square = square + three(dot_nt, (wh[l], wl[l]), (wh[l], wl[l]))
    sh[...], sl[...] = split(square)
    far_leaves(0)
    for xx in x_peers:
        remote(c1f.at[xx], c1f.at[xx], k1s.at[xx], k1r.at[xx], at(z, xx, c, y)).wait_recv()
        remote(si1.at[xx], si1.at[xx], i1s.at[xx], i1r.at[xx], at(z, xx, c, y)).wait_recv()
    for zz in z_peers:
        remote(c2f.at[zz], c2f.at[zz], k2s.at[zz], k2r.at[zz], at(zz, x, c, y)).wait_recv()
        remote(si2.at[zz], si2.at[zz], i2s.at[zz], i2r.at[zz], at(zz, x, c, y)).wait_recv()
    for m in range(XN):
        c1h[m], c1l[m] = split(c1f[m])
    for m in range(ZN):
        c2h[m], c2l[m] = split(c2f[m])
    partials(0)
    near(0)
    up = product(dot_nt, stacked(acc[0]), wh[0], wl[0])
    for l in range(1, LEAF):
        up = up + product(dot_nt, stacked(acc[l]), wh[l], wl[l])
    down = from_above(0)

    send_up(1, up + product(dot_nn, down, sh[...], sl[...]))
    finish(0, down)
    coefs(1)
    for side in range(2):
        coef_copy(1, side).start()
    send_halo(1)
    near_own()
    group(1)
    far_leaves(1)
    partials(1)
    near(1)
    finish(1, from_above(1))

    for pair in coupling_copies():
        for cp in pair:
            cp.wait_send()
    for p in range(2):
        for side in range(2):
            for i in range(LEAF):
                halo(p, side, i).wait_send()
            coef_copy(p, side).wait_send()
        for yy in y_peers:
            y_copy(p, yy, y).wait_send()
        for zz in z_peers:
            pz_copy(p, zz, z).wait_send()
            for yy in every_y:
                z_copy(p, zz, yy, z, y).wait_send()
        for xx in x_peers:
            px_copy(p, xx, x).wait_send()
            for yy in every_y:
                g_copy(p, xx, yy, x, y).wait_send()
        for zz in [z] + z_peers:
            forward(p, zz).wait_send()
        forward_top(p).wait_send()
        for l in range(LEAF):
            write(p, l).wait()


def hand_over(a, b, first, second, sem):
    copies = [pltpu.make_async_copy(a, first, sem.at[0]), pltpu.make_async_copy(b, second, sem.at[1])]
    for cp in copies:
        cp.start()
    for cp in copies:
        cp.wait()


def solution(mesh):
    leaf, grp = ("leaf", "grp")
    YN = mesh.shape[grp]
    XN = ZN = math.isqrt(mesh.shape[leaf] // 2)
    both = (leaf, grp)
    placed = (
        P(None, both),
        P(both, None),
        P(both, None, None, None),
        P(both, None, None),
        P(both, None),
        P(both, None, None, None),
        P(both, None, None),
        P(both, None, None),
        P(both, None),
        P(both, None, None, None),
        P(leaf, None),
        P(leaf, None, None, None),
    )

    def body(*refs):
        return kernel(ZN, XN, YN, *refs)

    hbm = pl.BlockSpec(memory_space=pl.ANY)
    anywhere = pl.BlockSpec(memory_space=pl.ANY)
    vmem = pltpu.VMEM
    dma = pltpu.SemaphoreType.DMA
    cols = LEAF * NODE
    scratch = [
        vmem((3, LEAF, RHS, NODE), F32),
        vmem((3 * LEAF, 2 * RHS, NODE), BF16),
        vmem((2, 2, LEAF, RHS, NODE), F32),
        vmem((LEAF, NEAR, NODE, NODE), F32),
        vmem((LEAF, NEAR, NODE, NODE), BF16),
        vmem((LEAF, NEAR, NODE, NODE), BF16),
        vmem((LEAF, RANK, NODE), F32),
        vmem((LEAF, RANK, NODE), BF16),
        vmem((LEAF, RANK, NODE), BF16),
        vmem((LEAF, LANES, NODE), BF16),
        vmem((LEAF, LANES, NODE), BF16),
        vmem((LANES, LANES), BF16),
        vmem((LANES, LANES), BF16),
        vmem((LEAF, RANK, RANK), F32),
        vmem((RANK, RANK), F32),
        vmem((LEAF, FAR, RANK, RANK), F32),
        vmem((LEAF, RANK, WIDE), BF16),
        vmem((LEAF, RANK, WIDE), BF16),
        vmem((FAR, RANK, RANK), F32),
        vmem((FAR, RANK, RANK), F32),
        vmem((XN, RANK, WIDE), F32),
        vmem((XN, RANK, WIDE), BF16),
        vmem((XN, RANK, WIDE), BF16),
        vmem((ZN, RANK, WIDE), F32),
        vmem((ZN, RANK, WIDE), BF16),
        vmem((ZN, RANK, WIDE), BF16),
        vmem((2, YN, 2, PACK, LANES), F32),
        vmem((2, XN, YN, PACK, LANES), F32),
        vmem((2, ZN, YN, PACK, LANES), F32),
        vmem((2, ZN, YN, PACK, LANES), F32),
        vmem((2, XN, PACK, LANES), F32),
        vmem((2, XN, PACK, LANES), F32),
        vmem((2, XN, PACK, LANES), F32),
        vmem((2, XN, PACK, LANES), F32),
        vmem((2, ZN, PACK, LANES), F32),
        vmem((2, ZN, PACK, LANES), F32),
        vmem((2, LEAF // 2, RHS, 2 * RANK), F32),
        vmem((2, 2, LEAF // 2, RHS, 2 * RANK), F32),
        vmem((3 * LEAF, RHS, 2 * RANK), F32),
        vmem((LEAF, RHS, NODE), F32),
        pltpu.SMEM((NEAR, LEAF), jnp.int32),
        pltpu.SMEM((LEAF, FAR), jnp.int32),
        pltpu.SMEM((XN, 1, FAR), jnp.int32),
        pltpu.SMEM((ZN, 1, FAR), jnp.int32),
        dma((10,)), dma((LEAF,)), dma((LEAF,)), dma((2, LEAF)),
        dma((2, 2, LEAF)), dma((2, 2, LEAF)),
        dma((2, 2)), dma((2, 2)),
        dma((2, YN)), dma((2, YN)),
        dma((2, ZN, YN)), dma((2, ZN, YN)),
        dma((2, XN, YN)), dma((2, XN, YN)),
        dma((2, ZN)), dma((2, ZN)), dma((2,)), dma((2,)),
        dma((2, XN)), dma((2, XN)),
        dma((2, ZN)), dma((2, ZN)),
        dma((XN,)), dma((XN,)), dma((ZN,)), dma((ZN,)),
        dma((XN,)), dma((XN,)), dma((ZN,)), dma((ZN,)),
    ]

    def per_device(signal, near_index, near_block, basis, *rest):
        args = (signal, near_index.T, near_block, jnp.swapaxes(basis, 1, 2), *rest)
        call = pl.pallas_call(
            body,
            out_shape=[jax.ShapeDtypeStruct((RHS, cols), F32)] * 2,
            in_specs=[hbm] * 12,
            out_specs=[anywhere, anywhere],
            scratch_shapes=scratch,
            compiler_params=pltpu.CompilerParams(
                collective_id=0, has_side_effects=True, vmem_limit_bytes=56 * 1024 * 1024
            ),
        )
        images = call(*args)
        final = pl.pallas_call(
            hand_over,
            out_shape=[jax.ShapeDtypeStruct((RHS, cols), F32)] * 2,
            in_specs=[pl.BlockSpec(memory_space=vmem)] * 2,
            out_specs=[hbm, hbm],
            scratch_shapes=[dma((2,))],
        )
        return tuple(final(*images))

    return jax.shard_map(
        per_device,
        mesh=mesh,
        in_specs=placed,
        out_specs=(P(None, both), P(None, both)),
        check_vma=False,
    )
```
